128 devices in a mesh: grp: 4 (over x_lo, core), dev: 32 (over z, y, x_hi).
Axes of the slice: x: 4 (x_hi: 2, x_lo: 2; x = x_hi * 2 + x_lo), y: 4, z: 4, core: 2. Of those that a mesh axis runs over, the one named last changes fastest.
Arguments:
- views_a: bfloat16 [32768, 256], P(('grp', 'dev')), may hold values from -6 to 6
- views_b: bfloat16 [32768, 256], P(('grp', 'dev')), may hold values from -6 to 6
- positives: int32 [32768], P(('grp', 'dev')), may hold values from 0 to 32767, as said below
- plan: int32 [2, 4], replicated, may hold values from 0 to 3, as said below
Outputs:
- grad_a: float32 [32768, 256], P(('grp', 'dev'))
- grad_b: float32 [32768, 256], P(('grp', 'dev'))
The draws below stay inside these ranges and needn't reach their ends.
Inputs may be any that keep to these rules, and one draw needn't show every extreme that they name: Row r holds a round of one round-robin over the 4 groups: plan[r, plan[r, g]] == g and plan[r, g] != g; no two rows pair the same two groups. positives[i] is i itself or a view of a group that plan pairs with the group of view i in some row.
All inputs are finite; a program needn't handle non-finite values.
Results may differ from the reference program's by a relative error of at most 0.00057.
Values may be sent and summed in bfloat16 or wider, within the bound.
No kernel may reach another device: no remote copies, remote signals or barrier semaphores. Data moves between devices by JAX's collectives and lax.ppermute only.
A program may use at most 128 MiB of HBM per device.

```python
import math
import jax
import jax.numpy as jnp
from jax import lax

D = 256
ROWS_DEV = 256
ROUNDS = 2
GROUPS = 4
GROUP_ROWS = 8192
VIEWS = 32768


def round_table(key):
    perm_key, pick_key = jax.random.split(key)
    players = GROUPS - 1
    labels = jax.random.permutation(perm_key, GROUPS).astype(jnp.int32)
    chosen = jax.random.permutation(pick_key, players).astype(jnp.int32)
    seats = jnp.arange(GROUPS, dtype=jnp.int32)
    table_rows = []
    for slot in range(ROUNDS):
        picked = chosen[slot]
        mates = (2 * picked - seats) % players
        mates = jnp.where(mates == seats, players, mates)
        mates = jnp.where(seats == players, picked, mates)
        table_rows.append(jnp.zeros((GROUPS,), jnp.int32).at[labels].set(labels[mates]))
    return jnp.stack(table_rows).astype(jnp.int32)


def draw_plan(key, part):
    return round_table(key)


def draw_positives(key, part):
    table = round_table(key)
    key = jax.random.fold_in(key, 7)
    which_key, row_key = jax.random.split(key)
    views = jnp.arange(VIEWS, dtype=jnp.int32)
    group = views // GROUP_ROWS
    which = jax.random.randint(which_key, (VIEWS,), 0, ROUNDS + 1).astype(jnp.int32)
    which = which.at[VIEWS - 1].set(0).at[0].set(0)
    partner = table[jnp.clip(which - 1, 0, ROUNDS - 1), group]
    local = jax.random.randint(row_key, (VIEWS,), 0, GROUP_ROWS).astype(jnp.int32)
    return jnp.where(which == 0, views, partner * GROUP_ROWS + local).astype(jnp.int32)


def shard_levels(stream_key, dims, pieces, smallest, top_value):
    level, own = 1.0, jax.random.fold_in(stream_key, 6)
    for position, blocks in pieces:
        heights = jnp.exp(jax.random.uniform(jax.random.fold_in(own, position), (blocks,), jnp.float32, smallest / len(pieces), top_value / len(pieces)))
        level = level * jnp.repeat(heights, dims[position] // blocks).reshape([-1 if axis == position else 1 for axis in range(len(dims))])
    return level


def noise(own_key, shape, spread, reach, shards=(), held_as=jnp.bfloat16):
    factor_of = shard_levels(own_key, shape, shards, -0.22, 0.18) if shards else 1.0
    drawn = jax.random.normal(own_key, shape, jnp.float32) * spread * factor_of
    return jnp.minimum(jnp.maximum(drawn, -reach), reach).astype(held_as)


def setup_inputs(seed: int = 0) -> dict:
    key_of = jax.random.split(jax.random.key(seed), 5)
    views_a = noise(key_of[0], (VIEWS, D), 1.0, 6.0, ((0, 128),))
    views_b = noise(key_of[1], (VIEWS, D), 1.0, 6.0, ((0, 128),))
    positives = draw_positives(jax.random.fold_in(key_of[4], 71), 0)
    plan = draw_plan(jax.random.fold_in(key_of[4], 71), 0)
    return dict(views_a=views_a, views_b=views_b, positives=positives, plan=plan)


logit_scale = 2.0
logit_bias = -6.0

def reference(views_a, views_b, positives, plan):
    factor = logit_scale / math.sqrt(D)
    blocks = VIEWS // ROWS_DEV

    def step(grad_b, index):
        start = (index * ROWS_DEV).astype(jnp.int32)
        group = (start // GROUP_ROWS).astype(jnp.int32)
        queries = lax.dynamic_slice_in_dim(views_a, start, ROWS_DEV, 0)
        labels = lax.dynamic_slice_in_dim(positives, start, ROWS_DEV, 0)
        owners = jnp.concatenate([group[None], plan[:, group].astype(jnp.int32)])
        grad_block = jnp.zeros((ROWS_DEV, D), jnp.float32)
        for slot in range(ROUNDS + 1):
            first = (owners[slot] * GROUP_ROWS).astype(jnp.int32)
            keys = lax.dynamic_slice_in_dim(views_b, first, GROUP_ROWS, 0)
            logits = jnp.dot(queries, keys.T, preferred_element_type=jnp.float32) * factor + logit_bias
            columns = first + jnp.arange(GROUP_ROWS, dtype=jnp.int32)
            hit = (labels[:, None] == columns[None, :]).astype(jnp.float32)
            weights = (jax.nn.sigmoid(logits) - hit).astype(jnp.bfloat16)
            grad_block = grad_block + jnp.dot(weights, keys, preferred_element_type=jnp.float32)
            part = jnp.dot(weights.T, queries, preferred_element_type=jnp.float32)
            current = lax.dynamic_slice_in_dim(grad_b, first, GROUP_ROWS, 0)
            grad_b = lax.dynamic_update_slice_in_dim(grad_b, current + part, first, 0)
        return (grad_b, grad_block)
    grad_b, grad_blocks = lax.scan(step, jnp.zeros((VIEWS, D), jnp.float32), jnp.arange(blocks, dtype=jnp.int32))
    return (grad_blocks.reshape(VIEWS, D) * factor, grad_b * factor)
```

```python
import functools
import math

import jax
import jax.numpy as jnp
from jax import lax
from jax.experimental import pallas as pl
from jax.experimental.pallas import tpu as pltpu
from jax.sharding import Mesh, PartitionSpec as P

logit_scale = 2.0
logit_bias = -6.0
AXES = ("xl", "core", "z", "y", "xh")
ROWS = 256
NOTE = 16


def x_place(x):
    return (x % 2) * 2 + (x // 2) % 2


def along_x(value, shift):
    pairs = [(x_place(x), x_place((x + shift) % 4)) for x in range(4)]
    return lax.ppermute(value, ("xl", "xh"), pairs)


def along_y(value, shift):
    return lax.ppermute(value, "y", [(y, (y + shift) % 4) for y in range(4)])


def swap_low(value):
    return lax.ppermute(value, "z", [(z, z ^ 1) for z in range(4)])


def swap_far(value):
    return lax.ppermute(value, "z", [(z, 3 - z) for z in range(4)])


def swap_core(value):
    return lax.ppermute(value, "core", [(0, 1), (1, 0)])


def gather_ring(shift, pair):
    half = pair.shape[0] // 2
    before = shift(pair, 1)
    after = shift(pair, -1)
    first = shift(before[:half], 1)
    second = shift(after[half:], -1)
    return before, after, first, second


def scatter_ring(shift, own, before, after, opposite):
    half = opposite.shape[0] // 2
    from_before = shift(opposite[:half], 1)
    from_after = shift(opposite[half:], -1)
    after = jnp.concatenate([after[:half] + from_before, after[half:]])
    before = jnp.concatenate([before[:half], before[half:] + from_after])
    return own + shift(after, 1) + shift(before, -1)


def kernel(factor, marks, *refs):
    a_refs, b_refs = refs[:5], refs[5:15]
    ga_ref, gb_ref, a_all, labels, b_all = refs[15:]
    step = ROWS + NOTE
    chunk = 0
    for ref in a_refs:
        for start in range(0, ref.shape[0], step):
            a_all[pl.ds(chunk * ROWS, ROWS), :] = ref[start : start + ROWS, :]
            note = ref[start + ROWS : start + step, :].astype(jnp.float32)
            labels[:, pl.ds(chunk * ROWS, ROWS)] = (note[0:1] * 256.0 + note[1:2]).astype(jnp.int32)
            chunk += 1
    for core in range(2):
        own, before, after, first, second = b_refs[5 * core : 5 * core + 5]
        same, other = core, 2 + core
        b_all[same, 0:512, :] = own[...]
        b_all[same, 512:768, :] = first[...]
        b_all[same, 768:1024, :] = second[...]
        b_all[other, 0:512, :] = before[...]
        b_all[other, 512:1024, :] = after[...]
    ga_ref[...] = jnp.zeros_like(ga_ref)
    gb_ref[marks[3]] = jnp.zeros((4 * ROWS, ROWS), jnp.float32)
    half_scale = 0.5 * factor
    half_bias = 0.5 * logit_bias
    iota = lax.broadcasted_iota(jnp.int32, (ROWS, 8 * ROWS), 0)

    def block(index, carry):
        slot = index // 4
        part = index % 4
        which = marks[slot]
        rows = pl.ds(pl.multiple_of(part * ROWS, ROWS), ROWS)
        keys = b_all[which, rows, :]
        a = a_all[...]
        logits = lax.dot_general(
            keys, a, (((1,), (1,)), ((), ())), preferred_element_type=jnp.float32
        )
        hit = iota == labels[...] - marks[4 + which * 4 + part]
        weights = 0.5 * jnp.tanh(logits * half_scale + half_bias) + jnp.where(hit, -0.5, 0.5)
        weights = weights.astype(jnp.bfloat16)
        gb_ref[which, rows, :] = jnp.dot(weights, a, preferred_element_type=jnp.float32)
        ga_ref[...] += lax.dot_general(
            weights, keys, (((0,), (0,)), ((), ())), preferred_element_type=jnp.float32
        )
        return carry

    lax.fori_loop(0, 12, block, 0)


def score(factor, marks, a_parts, b_parts):
    vmem = pl.BlockSpec(memory_space=pltpu.VMEM)
    return pl.pallas_call(
        functools.partial(kernel, factor),
        out_shape=(
            jax.ShapeDtypeStruct((8 * ROWS, ROWS), jnp.float32),
            jax.ShapeDtypeStruct((4, 4 * ROWS, ROWS), jnp.float32),
        ),
        in_specs=[pl.BlockSpec(memory_space=pltpu.SMEM)] + [vmem] * 15,
        out_specs=(vmem, vmem),
        scratch_shapes=[
            pltpu.VMEM((8 * ROWS, ROWS), jnp.bfloat16),
            pltpu.VMEM((1, 8 * ROWS), jnp.int32),
            pltpu.VMEM((4, 4 * ROWS, ROWS), jnp.bfloat16),
        ],
        compiler_params=pltpu.CompilerParams(vmem_limit_bytes=48 << 20),
        cost_estimate=pl.CostEstimate(
            flops=2 * 3 * 2048 * 3072 * 256, bytes_accessed=10 << 20, transcendentals=2048 * 3072
        ),
    )(marks, *a_parts, *b_parts)


def shards(views_a, views_b, positives, plan):
    factor = logit_scale / math.sqrt(views_a.shape[1])
    xl, core = lax.axis_index("xl"), lax.axis_index("core")
    z, y, xh = lax.axis_index("z"), lax.axis_index("y"), lax.axis_index("xh")
    group = xl * 2 + core
    first, second = plan[0, group] ^ group, plan[1, group] ^ group
    unused = first ^ second
    x = xh * 2 + xl
    places = {}
    for offset in range(4):
        at = (x + offset) % 4
        for far in range(2):
            zz = jnp.where(far == 1, 3 - z, z)
            places[offset, far] = (at % 2) * 16384 + (zz * 8 + y * 2 + at // 2) * 256
    bases = []
    for which in range(4):
        other = core if which % 2 == 0 else 1 - core
        if which < 2:
            order = [(0, 0), (0, 1), (2, 0), (2, 1)]
        else:
            order = [(3, 0), (3, 1), (1, 0), (1, 1)]
        bases += [places[o] + other * 8192 for o in order]
    zero = jnp.int32(0)
    marks = jnp.stack([v.astype(jnp.int32) for v in [zero, first, second, unused] + bases])

    note = jnp.stack([positives // 256, positives % 256]).astype(jnp.bfloat16)
    note = jnp.pad(note, ((0, NOTE - 2), (0, 0)))
    a_own = jnp.concatenate([views_a, note])
    a_own = jnp.concatenate([a_own, swap_low(a_own)])
    b_own = jnp.concatenate([views_b, swap_far(views_b)])
    a_parts = [a_own, *gather_ring(along_y, a_own)]
    b_parts = [b_own, *gather_ring(along_x, b_own)]
    b_parts += [swap_core(part) for part in b_parts]
    grad_a, grad_b = score(factor, marks, a_parts, b_parts)

    step = 2 * ROWS
    a_own, a_before, a_after, a_opposite = [grad_a[i * step : (i + 1) * step] for i in range(4)]
    a_mine = scatter_ring(along_y, a_own, a_before, a_after, a_opposite)
    grad_a = a_mine[:ROWS] + swap_low(a_mine[ROWS:])

    got = swap_core(jnp.stack([grad_b[1], grad_b[3]]))
    same, other = grad_b[0] + got[0], grad_b[2] + got[1]
    b_mine = scatter_ring(along_x, same[:step], other[:step], other[step:], same[step:])
    grad_b = b_mine[:ROWS] + swap_far(b_mine[ROWS:])
    return grad_a * factor, grad_b * factor


def solution(mesh):
    fine = Mesh(mesh.devices.reshape(2, 2, 4, 4, 2), AXES)
    split = P(AXES, None)
    return jax.shard_map(
        shards,
        mesh=fine,
        in_specs=(split, split, P(AXES), P()),
        out_specs=(split, split),
        check_vma=False,
    )
```

```python
import functools
import math

import jax
import jax.numpy as jnp
from jax import lax
from jax.experimental import pallas as pl
from jax.experimental.pallas import tpu as pltpu
from jax.sharding import Mesh, PartitionSpec as P

logit_scale = 2.0
logit_bias = -6.0
AXES = ("xl", "core", "z", "y", "xh")
ROWS = 256
NOTE = 16
PEAK = 32000.0
VMEM = pl.BlockSpec(memory_space=pltpu.VMEM)
SMEM = pl.BlockSpec(memory_space=pltpu.SMEM)


def member(xl, core, z, y, xh):
    return (((xl * 2 + core) * 4 + z) * 4 + y) * 2 + xh


def teams():
    out = []
    for pair in ((0, 1), (2, 3)):
        for x in range(4):
            out.append([member(x % 2, 0, z, y, x // 2) for z in pair for y in range(4)])
    for pair in ((0, 3), (1, 2)):
        for y in range(4):
            out.append([member(x % 2, 1, z, y, x // 2) for z in pair for x in range(4)])
    return out


def meet(value):
    return lax.all_to_all(value, AXES, 0, 0, axis_index_groups=teams(), tiled=True)


def swap_core(value):
    return lax.ppermute(value, "core", [(0, 1), (1, 0)])


def encode(block):
    top = jnp.maximum(jnp.max(jnp.abs(block), axis=0, keepdims=True), 2.0**-100)
    power = jnp.ceil(jnp.log2(top) * 128.0) + 1.0
    scaled = block * (PEAK * jnp.exp2(power * (-1.0 / 128.0)))
    return jnp.floor(scaled + 0.5).astype(jnp.int16), power


def decode(code, power):
    return code.astype(jnp.float32) * (jnp.exp2(power * (1.0 / 128.0)) * (1.0 / PEAK))


def notes(powers):
    powers = powers + [jnp.zeros((1, ROWS), jnp.float32)] * (NOTE - len(powers))
    return jnp.concatenate(powers, axis=0).astype(jnp.int16)


def source_of(marks, base, index):
    group = marks[base + index // 4]
    x = (index // 2) % 2 * 2 + group // 2
    return group, index % 2 * 4 + x


def score_kernel(factor, marks, mine, theirs, keep, send, a_all, labels, b_all, ga, gb):
    core, z, y = marks[0], marks[1], marks[2]

    def fill(a_from, a_start, b_from):
        for s in range(8):
            a_all[s * ROWS : (s + 1) * ROWS, :] = a_from[s, a_start : a_start + ROWS, :]
            note = a_from[s, a_start + ROWS : a_start + ROWS + NOTE, :].astype(jnp.float32)
            labels[:, s * ROWS : (s + 1) * ROWS] = (note[0:1] * 256.0 + note[1:2]).astype(jnp.int32)
            for c in range(2):
                start = c * (ROWS + NOTE)
                b_all[2 * s + c] = b_from[s, start : start + ROWS, :]

    @pl.when(core == 0)
    def _():
        fill(mine, 0, theirs)

    @pl.when(core == 1)
    def _():
        fill(theirs, ROWS + NOTE, mine)

    ga[...] = jnp.zeros_like(ga)
    half_scale = 0.5 * factor
    half_bias = 0.5 * logit_bias
    iota = lax.broadcasted_iota(jnp.int32, (ROWS, 8 * ROWS), 0)

    def block(index, carry):
        group, source = source_of(marks, 3, index)
        outer = jnp.logical_or(z == 0, z == 3)
        far = source // 4
        level = jnp.where(outer, 3 * far, 1 + far)
        first = group * 8192 + (level * 8 + y * 2 + source % 4 // 2) * ROWS
        which = source * 2 + group % 2
        keys = b_all[which]
        a = a_all[...]
        logits = lax.dot_general(
            keys, a, (((1,), (1,)), ((), ())), preferred_element_type=jnp.float32
        )
        hit = iota == labels[...] - first
        weights = 0.5 * jnp.tanh(logits * half_scale + half_bias) + jnp.where(hit, -0.5, 0.5)
        weights = weights.astype(jnp.bfloat16)
        gb[index] = jnp.dot(weights, a, preferred_element_type=jnp.float32)
        ga[...] += lax.dot_general(
            weights, keys, (((0,), (0,)), ((), ())), preferred_element_type=jnp.float32
        )
        return carry

    lax.fori_loop(0, 12, block, 0)

    @pl.when(core == 0)
    def _():
        powers = []
        for i in range(12):
            code, power = encode(gb[i])
            send[i * ROWS : (i + 1) * ROWS, :] = code
            powers.append(power)
        send[12 * ROWS :, :] = notes(powers)
        for i in range(8):
            keep[i] = ga[i * ROWS : (i + 1) * ROWS, :]

    @pl.when(core == 1)
    def _():
        powers = []
        for i in range(8):
            code, power = encode(ga[i * ROWS : (i + 1) * ROWS, :])
            send[i * ROWS : (i + 1) * ROWS, :] = code
            powers.append(power)
        send[12 * ROWS :, :] = notes(powers)
        for i in range(12):
            keep[i] = gb[i]


def pack_kernel(marks, keep, got, out, total):
    core = marks[0]

    @pl.when(core == 0)
    def _():
        for s in range(8):
            code, power = encode(keep[s])
            out[s, 0:ROWS, :] = code
            out[s, ROWS : 2 * ROWS, :] = got[s * ROWS : (s + 1) * ROWS, :]
            other = got[12 * ROWS :, :].astype(jnp.float32)[s : s + 1]
            out[s, 2 * ROWS :, :] = notes([power, other])

    @pl.when(core == 1)
    def _():
        for group in range(4):
            for i in range(4):
                total[group * 4 + i] = jnp.zeros((ROWS, ROWS), jnp.float32)
        for i in range(12):
            group = marks[3 + i // 4]
            total[group * 4 + i % 4] += keep[i]
        powers = got[12 * ROWS :, :].astype(jnp.float32)
        for i in range(12):
            group = marks[7 + i // 4]
            total[group * 4 + i % 4] += decode(got[i * ROWS : (i + 1) * ROWS, :], powers[i : i + 1])
        for s in range(8):
            x, far = s % 4, s // 4
            powers = []
            for c in range(2):
                code, power = encode(total[(x % 2 * 2 + c) * 4 + x // 2 * 2 + far])
                out[s, c * ROWS : (c + 1) * ROWS, :] = code
                powers.append(power)
            out[s, 2 * ROWS :, :] = notes(powers)


def sum_kernel(factor, marks, got, keep, send):
    core = marks[0]
    sums = [jnp.zeros((ROWS, ROWS), jnp.float32) for _ in range(2)]
    for s in range(8):
        powers = got[s, 2 * ROWS :, :].astype(jnp.float32)
        for c in range(2):
            sums[c] += decode(got[s, c * ROWS : (c + 1) * ROWS, :], powers[c : c + 1])
    first, second = sums[0] * factor, sums[1] * factor
    keep[...] = jnp.where(core == 0, first, second)
    send[...] = jnp.where(core == 0, second, first)


def call(kernel, shapes, scratch, flops, *operands):
    return pl.pallas_call(
        kernel,
        out_shape=shapes,
        in_specs=[SMEM] + [VMEM] * (len(operands) - 1),
        out_specs=jax.tree.map(lambda _: VMEM, shapes),
        scratch_shapes=scratch,
        compiler_params=pltpu.CompilerParams(vmem_limit_bytes=40 << 20),
        cost_estimate=pl.CostEstimate(flops=flops, bytes_accessed=8 << 20, transcendentals=0),
    )(*operands)


def shards(views_a, views_b, positives, plan):
    factor = logit_scale / math.sqrt(views_a.shape[1])
    xl, core = lax.axis_index("xl"), lax.axis_index("core")
    group = xl * 2 + core
    mate = group ^ 1
    marks = [core, lax.axis_index("z"), lax.axis_index("y")]
    marks += [group, plan[0, group], plan[1, group], group, mate, plan[0, mate], plan[1, mate]]
    marks = jnp.stack([v.astype(jnp.int32) for v in marks])

    note = jnp.stack([positives // 256, positives % 256]).astype(jnp.bfloat16)
    note = jnp.pad(note, ((0, NOTE - 2), (0, 0)))
    a_own = jnp.concatenate([views_a, note])
    b_own = jnp.pad(views_b, ((0, NOTE), (0, 0)))
    got = swap_core(jnp.where(core == 0, b_own, a_own))
    one = jnp.where(core == 0, a_own, got)
    two = jnp.where(core == 0, got, b_own)
    pair = jnp.concatenate([one, two])
    mine = meet(jnp.tile(pair[None], (8, 1, 1)))
    theirs = swap_core(mine)

    f32, i16 = jnp.float32, jnp.int16
    keep, send = call(
        functools.partial(score_kernel, factor),
        (
            jax.ShapeDtypeStruct((12, ROWS, ROWS), f32),
            jax.ShapeDtypeStruct((12 * ROWS + NOTE, ROWS), i16),
        ),
        [
            pltpu.VMEM((8 * ROWS, ROWS), jnp.bfloat16),
            pltpu.VMEM((1, 8 * ROWS), jnp.int32),
            pltpu.VMEM((16, ROWS, ROWS), jnp.bfloat16),
            pltpu.VMEM((8 * ROWS, ROWS), f32),
            pltpu.VMEM((12, ROWS, ROWS), f32),
        ],
        2 * 3 * 2048 * 3072 * 256,
        marks,
        mine,
        theirs,
    )
    packed = call(
        pack_kernel,
        jax.ShapeDtypeStruct((8, 2 * ROWS + NOTE, ROWS), i16),
        [pltpu.VMEM((16, ROWS, ROWS), f32)],
        1 << 20,
        marks,
        keep,
        swap_core(send),
    )
    keep, send = call(
        functools.partial(sum_kernel, factor),
        (jax.ShapeDtypeStruct((ROWS, ROWS), f32), jax.ShapeDtypeStruct((ROWS, ROWS), f32)),
        [],
        1 << 20,
        marks,
        meet(packed),
    )
    got = swap_core(send)
    return jnp.where(core == 0, keep, got), jnp.where(core == 0, got, keep)


def solution(mesh):
    fine = Mesh(mesh.devices.reshape(2, 2, 4, 4, 2), AXES)
    split = P(AXES, None)
    return jax.shard_map(
        shards,
        mesh=fine,
        in_specs=(split, split, P(AXES), P()),
        out_specs=(split, split),
        check_vma=False,
    )
```

```python
import functools
import math

import jax
import jax.numpy as jnp
from jax import lax
from jax.experimental import pallas as pl
from jax.experimental.pallas import tpu as pltpu
from jax.sharding import Mesh, PartitionSpec as P

logit_scale = 2.0
logit_bias = -6.0
AXES = ("xl", "core", "z", "y", "xh")
ROWS = 256
NOTE = 16
PEAK = 32000.0
VMEM = pl.BlockSpec(memory_space=pltpu.VMEM)
SMEM = pl.BlockSpec(memory_space=pltpu.SMEM)


def member(xl, core, z, y, xh):
    return (((xl * 2 + core) * 4 + z) * 4 + y) * 2 + xh


def teams():
    out = []
    for pair in ((0, 1), (2, 3)):
        for x in range(4):
            out.append([member(x % 2, 0, z, y, x // 2) for z in pair for y in range(4)])
    for pair in ((0, 3), (1, 2)):
        for y in range(4):
            out.append([member(x % 2, 1, z, y, x // 2) for z in pair for x in range(4)])
    return out


def meet(value):
    return lax.all_to_all(value, AXES, 0, 0, axis_index_groups=teams(), tiled=True)


def swap_core(value):
    return lax.ppermute(value, "core", [(0, 1), (1, 0)])


def encode(block):
    top = jnp.maximum(jnp.max(jnp.abs(block), axis=0, keepdims=True), 2.0**-100)
    power = jnp.ceil(jnp.log2(top) * 128.0) + 1.0
    scaled = block * (PEAK * jnp.exp2(power * (-1.0 / 128.0)))
    return jnp.floor(scaled + 0.5).astype(jnp.int16), power


def decode(code, power):
    return code.astype(jnp.float32) * (jnp.exp2(power * (1.0 / 128.0)) * (1.0 / PEAK))


def notes(powers):
    powers = powers + [jnp.zeros((1, ROWS), jnp.float32)] * (NOTE - len(powers))
    return jnp.concatenate(powers, axis=0).astype(jnp.int16)


def build_kernel(marks, a, b, ids, a_got, b_got, ids_got, out):
    core = marks[0]

    def note(ref):
        value = ref[...]
        high, low = lax.shift_right_logical(value, 8), value & 255
        rows = [high.astype(jnp.float32), low.astype(jnp.float32)]
        rows += [jnp.zeros((NOTE - 2, ROWS), jnp.float32)]
        return jnp.concatenate(rows, axis=0).astype(jnp.bfloat16)

    def write(one, two, one_note, two_note):
        for s in range(8):
            out[s, 0:ROWS, :] = one[...]
            out[s, ROWS : ROWS + NOTE, :] = one_note
            out[s, ROWS + NOTE : 2 * ROWS + NOTE, :] = two[...]
            out[s, 2 * ROWS + NOTE :, :] = two_note

    @pl.when(core == 0)
    def _():
        write(a, a_got, note(ids), note(ids_got))

    @pl.when(core == 1)
    def _():
        nothing = jnp.zeros((NOTE, ROWS), jnp.bfloat16)
        write(b_got, b, nothing, nothing)


def score_kernel(factor, half, marks, mine, theirs, *refs):
    sums, send, a_all, labels, b_all = refs[-5:]
    core, z, y = marks[0], marks[1], marks[2]

    def fill(a_from, a_start, b_from):
        for s in range(a_from.shape[0]):
            a_all[s * ROWS : (s + 1) * ROWS, :] = a_from[s, a_start : a_start + ROWS, :]
            note = a_from[s, a_start + ROWS : a_start + ROWS + NOTE, :].astype(jnp.float32)
            labels[:, s * ROWS : (s + 1) * ROWS] = (note[0:1] * 256.0 + note[1:2]).astype(jnp.int32)
        for s in range(b_from.shape[0]):
            for c in range(2):
                start = c * (ROWS + NOTE)
                x, level = s % 4, s // 4
                to = (level * 4 + x % 2 * 2 + c) * 2 + x // 2
                b_all[to] = b_from[s, start : start + ROWS, :]

    @pl.when(core == 0)
    def _():
        fill(mine, 0, theirs)

    @pl.when(core == 1)
    def _():
        fill(theirs, ROWS + NOTE, mine)

    if half == 0:
        sums[...] = jnp.zeros_like(sums)
    else:
        sums[12:18] = jnp.zeros((6, ROWS, ROWS), jnp.float32)
    half_scale = 0.5 * factor
    half_bias = 0.5 * logit_bias
    wide, deep = 4 * ROWS, 2 * ROWS
    iota = lax.broadcasted_iota(jnp.int32, (deep, wide), 0)
    first = core == 0
    outer = jnp.logical_or(z == 0, z == 3)

    for tile in range(6):
        unit, slot = tile // 3, tile % 3
        group = marks[3 + slot]
        far = jnp.where(first, half, unit)
        level = jnp.where(outer, 3 * far, 1 + far)
        a_rows = pl.ds(pl.multiple_of(jnp.where(first, unit, 0) * wide, wide), wide)
        keys = b_all[pl.ds((jnp.where(first, 0, unit) * 4 + group) * 2, 2)].reshape(deep, ROWS)
        a = a_all[a_rows, :]
        ids = labels[:, a_rows]
        ids = jnp.where(lax.shift_right_logical(ids, 9) == group * 16 + level * 4 + y, ids & 511, -1)
        logits = lax.dot_general(
            keys, a, (((1,), (1,)), ((), ())), preferred_element_type=jnp.float32
        )
        weights = 0.5 * jnp.tanh(logits * half_scale + half_bias) + jnp.where(iota == ids, -0.5, 0.5)
        weights = weights.astype(jnp.bfloat16)
        gb = jnp.dot(weights, a, preferred_element_type=jnp.float32)
        ga = lax.dot_general(
            weights, keys, (((0,), (0,)), ((), ())), preferred_element_type=jnp.float32
        )
        gb_at = pl.ds(jnp.where(first, 12 + slot * 2, slot * 4 + unit * 2), 2)
        ga_at = pl.ds(jnp.where(first, unit * 4, 12), 4)
        sums[gb_at] += gb.reshape(2, ROWS, ROWS)
        sums[ga_at] += ga.reshape(4, ROWS, ROWS)

    powers = []
    for i in range(6):
        code, power = encode(sums[12 + i])
        send[i * ROWS : (i + 1) * ROWS, :] = code
        powers.append(power)
    send[6 * ROWS :, :] = notes(powers)


def place_in(marks, base, group):
    one, two = marks[base + 1] == group, marks[base + 2] == group
    used = jnp.logical_or(marks[base] == group, jnp.logical_or(one, two))
    return jnp.where(one, 1, jnp.where(two, 2, 0)), jnp.where(used, 1.0, 0.0)


def pack_kernel(marks, sums, got_near, got_far, out, total, powers):
    core = marks[0]
    for far, got in enumerate((got_near, got_far)):
        powers[far] = got[6 * ROWS :, :].astype(jnp.float32)

    @pl.when(core == 0)
    def _():
        for s in range(8):
            got, i = (got_near, got_far)[s // 4], s % 4
            code, power = encode(sums[s])
            out[s, 0:ROWS, :] = code
            out[s, ROWS : 2 * ROWS, :] = got[i * ROWS : (i + 1) * ROWS, :]
            out[s, 2 * ROWS :, :] = notes([power, powers[s // 4, i : i + 1, :]])

    @pl.when(core == 1)
    def _():
        for s in range(8):
            far, got = s // 4, (got_near, got_far)[s // 4]
            written = []
            for c in range(2):
                group, xh = s % 2 * 2 + c, s % 4 // 2
                own_slot, own_used = place_in(marks, 3, group)
                slot, used = place_in(marks, 6, group)
                own = sums[own_slot * 4 + far * 2 + xh]
                index = slot * 2 + xh
                power = powers[far, pl.ds(index, 1), :]
                scale = jnp.exp2(power * (1.0 / 128.0)) * (used * (1.0 / PEAK))
                code = got[pl.ds(pl.multiple_of(index * ROWS, ROWS), ROWS), :]
                total[...] = own * own_used + code.astype(jnp.float32) * scale
                code, power = encode(total[...])
                out[s, c * ROWS : (c + 1) * ROWS, :] = code
                written.append(power)
            out[s, 2 * ROWS :, :] = notes(written)


def sum_kernel(factor, marks, got, keep, send):
    core = marks[0]
    sums = [jnp.zeros((ROWS, ROWS), jnp.float32) for _ in range(2)]
    for s in range(8):
        powers = got[s, 2 * ROWS :, :].astype(jnp.float32)
        for c in range(2):
            sums[c] += decode(got[s, c * ROWS : (c + 1) * ROWS, :], powers[c : c + 1])
    first, second = sums[0] * factor, sums[1] * factor
    keep[...] = jnp.where(core == 0, first, second)
    send[...] = jnp.where(core == 0, second, first)


def call(kernel, shapes, scratch, flops, *operands, aliases={}):
    return pl.pallas_call(
        kernel,
        out_shape=shapes,
        in_specs=[SMEM] + [VMEM] * (len(operands) - 1),
        out_specs=jax.tree.map(lambda _: VMEM, shapes),
        scratch_shapes=scratch,
        input_output_aliases=aliases,
        compiler_params=pltpu.CompilerParams(vmem_limit_bytes=36 << 20),
        cost_estimate=pl.CostEstimate(flops=flops, bytes_accessed=8 << 20, transcendentals=0),
    )(*operands)


def shards(views_a, views_b, positives, plan):
    factor = logit_scale / math.sqrt(views_a.shape[1])
    xl, core = lax.axis_index("xl"), lax.axis_index("core")
    group = xl * 2 + core
    mate = group ^ 1
    marks = [core, lax.axis_index("z"), lax.axis_index("y"), group, plan[0, group], plan[1, group]]
    marks += [mate, plan[0, mate], plan[1, mate]]
    marks = jnp.stack([v.astype(jnp.int32) for v in marks])

    f32, i16, bf16 = jnp.float32, jnp.int16, jnp.bfloat16
    ids = positives.reshape(1, ROWS)
    shared = call(
        build_kernel,
        jax.ShapeDtypeStruct((8, 2 * (ROWS + NOTE), ROWS), bf16),
        [],
        1 << 20,
        marks,
        views_a,
        views_b,
        ids,
        swap_core(views_a),
        swap_core(views_b),
        swap_core(ids),
    )
    mine = meet(shared)
    near, far = swap_core(mine[:4]), swap_core(mine[4:])

    def score(half, theirs, *sums):
        return call(
            functools.partial(score_kernel, factor, half),
            (
                jax.ShapeDtypeStruct((18, ROWS, ROWS), f32),
                jax.ShapeDtypeStruct((6 * ROWS + NOTE, ROWS), i16),
            ),
            [
                pltpu.VMEM((8 * ROWS, ROWS), bf16),
                pltpu.VMEM((1, 8 * ROWS), jnp.int32),
                pltpu.VMEM((16, ROWS, ROWS), bf16),
            ],
            3 * 2048 * 3072 * 256,
            marks,
            mine,
            theirs,
            *sums,
            aliases={3: 0} if sums else {},
        )

    sums, send_near = score(0, near)
    got_near = swap_core(send_near)
    sums, send_far = score(1, far, sums)
    packed = call(
        pack_kernel,
        jax.ShapeDtypeStruct((8, 2 * ROWS + NOTE, ROWS), i16),
        [pltpu.VMEM((ROWS, ROWS), f32), pltpu.VMEM((2, NOTE, ROWS), f32)],
        1 << 20,
        marks,
        sums,
        got_near,
        swap_core(send_far),
    )
    keep, send = call(
        functools.partial(sum_kernel, factor),
        (jax.ShapeDtypeStruct((ROWS, ROWS), f32), jax.ShapeDtypeStruct((ROWS, ROWS), f32)),
        [],
        1 << 20,
        marks,
        meet(packed),
    )
    got = swap_core(send)
    return jnp.where(core == 0, keep, got), jnp.where(core == 0, got, keep)


def solution(mesh):
    fine = Mesh(mesh.devices.reshape(2, 2, 4, 4, 2), AXES)
    split = P(AXES, None)
    return jax.shard_map(
        shards,
        mesh=fine,
        in_specs=(split, split, P(AXES), P()),
        out_specs=(split, split),
        check_vma=False,
    )
```

```python
import functools
import math

import jax
import jax.numpy as jnp
from jax import lax
from jax.experimental import pallas as pl
from jax.experimental.pallas import tpu as pltpu
from jax.sharding import Mesh, PartitionSpec as P

logit_scale = 2.0
logit_bias = -6.0
AXES = ("xl", "core", "z", "y", "xh")
ROWS = 256
NOTE = 16
PEAK = 32000.0
VMEM = pl.BlockSpec(memory_space=pltpu.VMEM)
SMEM = pl.BlockSpec(memory_space=pltpu.SMEM)


def member(xl, core, z, y, xh):
    return (((xl * 2 + core) * 4 + z) * 4 + y) * 2 + xh


def teams():
    out = []
    for pair in ((0, 1), (2, 3)):
        for x in range(4):
            out.append([member(x % 2, 0, z, y, x // 2) for z in pair for y in range(4)])
    for pair in ((0, 3), (1, 2)):
        for y in range(4):
            out.append([member(x % 2, 1, z, y, x // 2) for z in pair for x in range(4)])
    return out


def meet(value):
    return lax.all_to_all(value, AXES, 0, 0, axis_index_groups=teams(), tiled=True)


def swap_core(value):
    return lax.ppermute(value, "core", [(0, 1), (1, 0)])


def encode(block):
    top = jnp.maximum(jnp.max(jnp.abs(block), axis=0, keepdims=True), 2.0**-100)
    power = jnp.ceil(jnp.log2(top) * 128.0) + 1.0
    scaled = block * (PEAK * jnp.exp2(power * (-1.0 / 128.0)))
    return jnp.floor(scaled + 0.5).astype(jnp.int16), power


def decode(code, power):
    return code.astype(jnp.float32) * (jnp.exp2(power * (1.0 / 128.0)) * (1.0 / PEAK))


def notes(powers):
    powers = powers + [jnp.zeros((1, ROWS), jnp.float32)] * (NOTE - len(powers))
    return jnp.concatenate(powers, axis=0).astype(jnp.int16)


def on_core(body):
    core = lax.axis_index("core")
    for number in range(2):
        pl.when(core == number)(functools.partial(body, number))


def window(plan, core):
    group = lax.axis_index("xl") * 2 + core
    return [group, plan[0, group], plan[1, group]]


def place_in(owners, group):
    hits = [owner == group for owner in owners]
    used = jnp.logical_or(hits[0], jnp.logical_or(hits[1], hits[2]))
    return jnp.where(hits[1], 1, jnp.where(hits[2], 2, 0)), jnp.where(used, 1.0, 0.0)


def build_kernel(a, b, ids, a_got, b_got, ids_got, out):
    def body(core):
        one, two = (a, a_got) if core == 0 else (b_got, b)
        rows = []
        for ref in (ids, ids_got) if core == 0 else ():
            value = ref[...]
            rows.append(lax.shift_right_logical(value, 8).astype(jnp.float32))
            rows.append((value & 255).astype(jnp.float32))
        rows.append(jnp.zeros((NOTE - len(rows), ROWS), jnp.float32))
        note = jnp.concatenate(rows, axis=0).astype(jnp.bfloat16)
        for s in range(8):
            out[s, 0:ROWS, :] = one[...]
            out[s, ROWS : 2 * ROWS, :] = two[...]
            out[s, 2 * ROWS :, :] = note

    on_core(body)


def score_kernel(factor, half, plan, mine, theirs, *refs):
    keep, send, sums = refs[-3:]
    half_scale = 0.5 * factor
    half_bias = 0.5 * logit_bias
    wide, deep = 4 * ROWS, 2 * ROWS
    z, y = lax.axis_index("z"), lax.axis_index("y")
    outer = jnp.logical_or(z == 0, z == 3)

    def add(ref, start, value, fresh):
        count = value.shape[0] // ROWS
        value = value.reshape(count, ROWS, ROWS)
        if not fresh:
            value = value + ref[start : start + count]
        ref[start : start + count] = value

    def body(core):
        owners = window(plan, core)
        for unit in range(2):
            a_from, a_source = (mine, 4 * unit) if core == 0 else (theirs, 0)
            a = [a_from[a_source + s, core * ROWS : (core + 1) * ROWS, :] for s in range(4)]
            a = jnp.concatenate(a, axis=0)
            ids = []
            for s in range(4):
                note = a_from[a_source + s, 2 * ROWS :, :].astype(jnp.float32)[2 * core : 2 * core + 2]
                ids.append((note[0:1] * 256.0 + note[1:2]).astype(jnp.int32))
            ids = jnp.concatenate(ids, axis=1)
            far = half if core == 0 else unit
            level = jnp.where(outer, 3 * far, 1 + far)
            for slot in range(3):
                group = owners[slot]
                b_from, b_source = (theirs, 0) if core == 0 else (mine, 4 * unit)
                b_rows = pl.ds(pl.multiple_of(group % 2 * ROWS, ROWS), ROWS)
                keys = [b_from[b_source + 2 * xh + group // 2, b_rows, :] for xh in range(2)]
                keys = jnp.concatenate(keys, axis=0)
                here = lax.shift_right_logical(ids, 9) == group * 16 + level * 4 + y
                rows = jnp.where(here, ids & 511, -1)
                hit = lax.broadcasted_iota(jnp.int32, (deep, wide), 0) == rows
                logits = lax.dot_general(
                    keys, a, (((1,), (1,)), ((), ())), preferred_element_type=jnp.float32
                )
                weights = 0.5 * jnp.tanh(logits * half_scale + half_bias) + jnp.where(hit, -0.5, 0.5)
                weights = weights.astype(jnp.bfloat16)
                gb = jnp.dot(weights, a, preferred_element_type=jnp.float32)
                ga = lax.dot_general(
                    weights, keys, (((0,), (0,)), ((), ())), preferred_element_type=jnp.float32
                )
                if core == 0:
                    add(sums, slot * 2, gb, unit == 0)
                    add(keep, unit * 4, ga, half == 0 and slot == 0)
                else:
                    add(keep, slot * 4 + unit * 2, gb, half == 0)
                    add(sums, 0, ga, unit == 0 and slot == 0)
        powers = []
        for i in range(6 if core == 0 else 4):
            code, power = encode(sums[i])
            send[i * ROWS : (i + 1) * ROWS, :] = code
            powers.append(power)
        send[6 * ROWS :, :] = notes(powers)

    on_core(body)


def pack_kernel(half, plan, keep, got, *refs):
    out, total, powers = refs[-3:]

    def body(core):
        if core == 0:
            got_powers = got[6 * ROWS :, :].astype(jnp.float32)
        else:
            powers[...] = got[6 * ROWS :, :].astype(jnp.float32)
            own, mate = window(plan, 1), window(plan, 0)
        for i in range(4):
            s = half * 4 + i
            written = []
            if core == 0:
                code, power = encode(keep[s])
                out[s, 0:ROWS, :] = code
                out[s, ROWS : 2 * ROWS, :] = got[i * ROWS : (i + 1) * ROWS, :]
                written = [power, got_powers[i : i + 1]]
            else:
                for c in range(2):
                    group, xh = i % 2 * 2 + c, i // 2
                    slot, kept = place_in(own, group)
                    value = keep[slot * 4 + half * 2 + xh] * kept
                    slot, used = place_in(mate, group)
                    index = slot * 2 + xh
                    scale = jnp.exp2(powers[pl.ds(index, 1), :] * (1.0 / 128.0)) * (used * (1.0 / PEAK))
                    code = got[pl.ds(pl.multiple_of(index * ROWS, ROWS), ROWS), :]
                    total[...] = value + code.astype(jnp.float32) * scale
                    code, power = encode(total[...])
                    out[s, c * ROWS : (c + 1) * ROWS, :] = code
                    written.append(power)
            out[s, 2 * ROWS :, :] = notes(written)

    on_core(body)


def sum_kernel(factor, got, keep, send):
    def body(core):
        for c in range(2):
            total = jnp.zeros((ROWS, ROWS), jnp.float32)
            for s in range(8):
                power = got[s, 2 * ROWS :, :].astype(jnp.float32)[c : c + 1]
                total += decode(got[s, c * ROWS : (c + 1) * ROWS, :], power)
            (keep if c == core else send)[...] = total * factor

    on_core(body)


def call(kernel, shapes, scratch, flops, *operands, plan=None, aliases={}):
    operands = operands if plan is None else (plan, *operands)
    return pl.pallas_call(
        kernel,
        out_shape=shapes,
        in_specs=[VMEM if plan is None or i else SMEM for i in range(len(operands))],
        out_specs=jax.tree.map(lambda _: VMEM, shapes),
        scratch_shapes=scratch,
        input_output_aliases=aliases,
        compiler_params=pltpu.CompilerParams(vmem_limit_bytes=36 << 20),
        cost_estimate=pl.CostEstimate(flops=flops, bytes_accessed=8 << 20, transcendentals=0),
    )(*operands)


def shards(views_a, views_b, positives, plan):
    factor = logit_scale / math.sqrt(views_a.shape[1])
    f32, i16, bf16 = jnp.float32, jnp.int16, jnp.bfloat16
    height = 2 * ROWS + NOTE
    ids = positives.reshape(1, ROWS)
    got = [swap_core(value) for value in (views_a, views_b, ids)]
    built = jax.ShapeDtypeStruct((8, height, ROWS), bf16)
    mine = meet(call(build_kernel, built, [], 1 << 20, views_a, views_b, ids, *got))
    near, far = swap_core(mine[:4]), swap_core(mine[4:])

    def score(half, theirs, *keep):
        return call(
            functools.partial(score_kernel, factor, half),
            (
                jax.ShapeDtypeStruct((12, ROWS, ROWS), f32),
                jax.ShapeDtypeStruct((6 * ROWS + NOTE, ROWS), i16),
            ),
            [pltpu.VMEM((6, ROWS, ROWS), f32)],
            3 * 2048 * 3072 * 256,
            mine,
            theirs,
            *keep,
            plan=plan,
            aliases={3: 0} if keep else {},
        )

    def pack(half, keep, got, *packed):
        return call(
            functools.partial(pack_kernel, half),
            jax.ShapeDtypeStruct((8, height, ROWS), i16),
            [pltpu.VMEM((ROWS, ROWS), f32), pltpu.VMEM((NOTE, ROWS), f32)],
            1 << 20,
            keep,
            got,
            *packed,
            plan=plan,
            aliases={3: 0} if packed else {},
        )

    keep, send_near = score(0, near)
    got_near = swap_core(send_near)
    keep, send_far = score(1, far, keep)
    got_far = swap_core(send_far)
    packed = pack(1, keep, got_far, pack(0, keep, got_near))
    one = jax.ShapeDtypeStruct((ROWS, ROWS), f32)
    keep, send = call(functools.partial(sum_kernel, factor), (one, one), [], 1 << 20, meet(packed))
    got = swap_core(send)
    core = lax.axis_index("core")
    return jnp.where(core == 0, keep, got), jnp.where(core == 0, got, keep)


def solution(mesh):
    fine = Mesh(mesh.devices.reshape(2, 2, 4, 4, 2), AXES)
    split = P(AXES, None)
    return jax.shard_map(
        shards,
        mesh=fine,
        in_specs=(split, split, P(AXES), P()),
        out_specs=(split, split),
        check_vma=False,
    )
```

```python
import functools
import math

import jax
import jax.numpy as jnp
from jax import lax
from jax.experimental import pallas as pl
from jax.experimental.pallas import tpu as pltpu
from jax.sharding import Mesh, PartitionSpec as P

logit_scale = 2.0
logit_bias = -6.0
AXES = ("xl", "core", "z", "y", "xh")
ROWS = 256
NOTE = 16
PEAK = 32000.0
VMEM = pl.BlockSpec(memory_space=pltpu.VMEM)
SMEM = pl.BlockSpec(memory_space=pltpu.SMEM)


def member(xl, core, z, y, xh):
    return (((xl * 2 + core) * 4 + z) * 4 + y) * 2 + xh


def teams():
    out = []
    for pair in ((0, 1), (2, 3)):
        for x in range(4):
            out.append([member(x % 2, 0, z, y, x // 2) for z in pair for y in range(4)])
    for pair in ((0, 3), (1, 2)):
        for y in range(4):
            out.append([member(x % 2, 1, z, y, x // 2) for z in pair for x in range(4)])
    return out


def step(value, level, shift):
    pairs = []
    for team in teams():
        for i in range(8):
            pairs.append((team[i], team[(i // 4 + level) % 2 * 4 + (i + shift) % 4]))
    return lax.ppermute(value, AXES, pairs)


def meet(value):
    return lax.all_to_all(value, AXES, 0, 0, axis_index_groups=teams(), tiled=True)


def swap_core(value):
    return lax.ppermute(value, "core", [(0, 1), (1, 0)])


def encode(block):
    top = jnp.maximum(jnp.max(jnp.abs(block), axis=0, keepdims=True), 2.0**-100)
    power = jnp.ceil(jnp.log2(top) * 128.0) + 1.0
    scaled = block * (PEAK * jnp.exp2(power * (-1.0 / 128.0)))
    return jnp.floor(scaled + 0.5).astype(jnp.int16), power


def decode(code, power):
    return code.astype(jnp.float32) * (jnp.exp2(power * (1.0 / 128.0)) * (1.0 / PEAK))


def notes(powers):
    powers = powers + [jnp.zeros((1, ROWS), jnp.float32)] * (NOTE - len(powers))
    return jnp.concatenate(powers, axis=0).astype(jnp.int16)


def on_core(body):
    core = lax.axis_index("core")
    for number in range(2):
        pl.when(core == number)(functools.partial(body, number))


def unused(plan):
    return plan[0, 0] ^ plan[1, 0]


def place(number, skip):
    return jnp.where(number == skip, 0, number - jnp.where(skip < number, 1, 0))


def build_kernel(own, ids, a_got, b_got, ids_got, out):
    def body(core):
        other = 1 - core
        out[core * ROWS : (core + 1) * ROWS, :] = own[...]
        out[other * ROWS : (other + 1) * ROWS, :] = (a_got if core == 0 else b_got)[...]
        rows = [ids[...].astype(jnp.float32), ids_got[...].astype(jnp.float32)]
        rows.append(jnp.zeros((NOTE - 4, ROWS), jnp.float32))
        out[2 * ROWS :, :] = jnp.concatenate(rows, axis=0).astype(jnp.bfloat16)

    on_core(body)


def score_kernel(factor, stage, plan, *refs):
    sets = [([0], [0]), ([1], [0]), ([0, 1], [1])][stage]
    mine = {which: refs[4 * i : 4 * i + 4] for i, which in enumerate(sets[0])}
    refs = refs[4 * len(sets[0]) :]
    theirs = {sets[1][0]: refs[:4]}
    if stage == 0:
        keep, sums = refs[4:]
        send = powers = None
    elif stage == 1:
        keep, sums, send, powers = refs[6:]
    else:
        keep, send, powers, sums = refs[5:]
    half_scale = 0.5 * factor
    half_bias = 0.5 * logit_bias
    wide, deep = 4 * ROWS, 2 * ROWS
    xl, xh = lax.axis_index("xl"), lax.axis_index("xh")
    z, y = lax.axis_index("z"), lax.axis_index("y")
    skip = unused(plan)

    def add(ref, start, value, fresh):
        count = value.shape[0] // ROWS
        value = value.reshape(count, ROWS, ROWS)
        if not fresh:
            value = value + ref[start : start + count]
        ref[start : start + count] = value

    def body(core):
        first, second = (mine, theirs) if core == 0 else (theirs, mine)
        for a_set, a_pieces in first.items():
            a = [piece[core * ROWS : (core + 1) * ROWS, :] for piece in a_pieces]
            a = jnp.concatenate(a, axis=0)
            ids = []
            for piece in a_pieces:
                note = piece[2 * ROWS :, :].astype(jnp.float32)[2 * core : 2 * core + 2]
                ids.append((note[0:1] * 256.0 + note[1:2]).astype(jnp.int32))
            ids = jnp.concatenate(ids, axis=1)
            for b_set, b_pieces in second.items():
                for number in range(4):
                    side = core ^ (number & 1)
                    offsets = (number // 2, number // 2 + 2)

                    def tile(number=number, side=side, offsets=offsets, a=a, ids=ids, a_set=a_set, b_set=b_set, b_pieces=b_pieces):
                        keys = [b_pieces[o][side * ROWS : (side + 1) * ROWS, :] for o in offsets]
                        keys = jnp.concatenate(keys, axis=0)
                        rows = jnp.full_like(ids, -1)
                        for place_of, o in enumerate(offsets):
                            x = (xh * 2 + xl + o) % 4
                            level = 3 - z if b_set else z
                            base = (x % 2 * 2 + side) * 32 + level * 8 + y * 2 + x // 2
                            here = lax.shift_right_logical(ids, 8) == base
                            rows = jnp.where(here, (ids & 255) + place_of * ROWS, rows)
                        hit = lax.broadcasted_iota(jnp.int32, (deep, wide), 0) == rows
                        logits = lax.dot_general(
                            keys, a, (((1,), (1,)), ((), ())), preferred_element_type=jnp.float32
                        )
                        weights = 0.5 * jnp.tanh(logits * half_scale + half_bias)
                        weights = (weights + jnp.where(hit, -0.5, 0.5)).astype(jnp.bfloat16)
                        gb = jnp.dot(weights, a, preferred_element_type=jnp.float32)
                        ga = lax.dot_general(
                            weights, keys, (((0,), (0,)), ((), ())), preferred_element_type=jnp.float32
                        )
                        if core == 0:
                            add(sums, number * 2, gb, stage == 0 or (stage == 2 and a_set == 0))
                            add(keep, a_set * 4, ga, stage < 2 and number == 0)
                        else:
                            add(keep, b_set * 8 + number * 2, gb, stage < 2)
                            add(sums, 0, ga, number == 0 and (stage == 0 or (stage == 2 and b_set == 0)))

                    if number:
                        pl.when(skip != number)(tile)
                    else:
                        tile()
        if stage == 0:
            return
        powers[...] = jnp.zeros_like(powers)
        for i in range(8 if core == 0 else 4):

            def write(i=i):
                code, power = encode(sums[i])
                at = place(i // 2, skip) * 2 + i % 2 if core == 0 else i
                send[pl.ds(pl.multiple_of(at * ROWS, ROWS), ROWS), :] = code
                powers[pl.ds(at, 1), :] = power

            if core == 0 and i > 1:
                pl.when(skip != i // 2)(write)
            else:
                write()
        send[6 * ROWS :, :] = powers[...].astype(jnp.int16)

    on_core(body)


def pack_kernel(far, plan, keep, got, *refs):
    out, total, powers = refs[-3:]
    z, y = lax.axis_index("z"), lax.axis_index("y")
    x = lax.axis_index("xh") * 2 + lax.axis_index("xl")
    skip = unused(plan)

    def body(core):
        if core == 0:
            got_powers = got[6 * ROWS :, :].astype(jnp.float32)
            level, at = z % 2, y
        else:
            powers[...] = got[6 * ROWS :, :].astype(jnp.float32)
            level, at = z // 2, x
        if far:
            level = 1 - level
        for o in range(4):
            s = level * 4 + (at + o) % 4
            written = []
            if core == 0:
                code, power = encode(keep[far * 4 + o])
                out[s, 0:ROWS, :] = code
                out[s, ROWS : 2 * ROWS, :] = got[o * ROWS : (o + 1) * ROWS, :]
                written = [power, got_powers[o : o + 1]]
            else:
                for c in range(2):
                    number = o % 2 * 2 + (1 - c)
                    value = jnp.where(skip != number, keep[far * 8 + number * 2 + o // 2], 0.0)
                    number = number ^ 1
                    used = jnp.where(skip != number, 1.0 / PEAK, 0.0)
                    index = place(number, skip) * 2 + o // 2
                    scale = jnp.exp2(powers[pl.ds(index, 1), :] * (1.0 / 128.0)) * used
                    code = got[pl.ds(pl.multiple_of(index * ROWS, ROWS), ROWS), :]
                    total[...] = value + code.astype(jnp.float32) * scale
                    code, power = encode(total[...])
                    out[s, c * ROWS : (c + 1) * ROWS, :] = code
                    written.append(power)
            out[s, 2 * ROWS :, :] = notes(written)

    on_core(body)


def sum_kernel(factor, got, keep, send):
    def body(core):
        for c in range(2):
            total = jnp.zeros((ROWS, ROWS), jnp.float32)
            for s in range(8):
                power = got[s, 2 * ROWS :, :].astype(jnp.float32)[c : c + 1]
                total += decode(got[s, c * ROWS : (c + 1) * ROWS, :], power)
            (keep if c == core else send)[...] = total * factor

    on_core(body)


def call(kernel, shapes, scratch, flops, *operands, plan=None, aliases={}):
    operands = operands if plan is None else (plan, *operands)
    return pl.pallas_call(
        kernel,
        out_shape=shapes,
        in_specs=[VMEM if plan is None or i else SMEM for i in range(len(operands))],
        out_specs=jax.tree.map(lambda _: VMEM, shapes),
        scratch_shapes=scratch,
        input_output_aliases=aliases,
        compiler_params=pltpu.CompilerParams(vmem_limit_bytes=36 << 20),
        cost_estimate=pl.CostEstimate(flops=flops, bytes_accessed=8 << 20, transcendentals=0),
    )(*operands)


def shards(views_a, views_b, positives, plan):
    factor = logit_scale / math.sqrt(views_a.shape[1])
    f32, i16, bf16 = jnp.float32, jnp.int16, jnp.bfloat16
    height = 2 * ROWS + NOTE
    core = lax.axis_index("core")
    ids = jnp.stack([positives // 256, positives % 256]).astype(bf16)
    got = [swap_core(value) for value in (views_a, views_b, ids)]
    shared = jnp.where(core == 0, views_a, views_b)
    piece = jax.ShapeDtypeStruct((height, ROWS), bf16)
    own = call(build_kernel, piece, [], 1 << 10, shared, ids, *got)
    over = step(own, 1, 0)
    near = [own, step(own, 0, 3), step(own, 0, 2), step(own, 0, 1)]
    far = [over, step(over, 0, 3), step(over, 0, 2), step(over, 0, 1)]
    near_mate = [swap_core(piece) for piece in near]

    keep_shape = jax.ShapeDtypeStruct((16, ROWS, ROWS), f32)
    sums_shape = jax.ShapeDtypeStruct((8, ROWS, ROWS), f32)
    send_shape = jax.ShapeDtypeStruct((6 * ROWS + NOTE, ROWS), i16)
    powers = pltpu.VMEM((NOTE, ROWS), f32)

    def score(stage, shapes, scratch, *operands, aliases={}):
        return call(
            functools.partial(score_kernel, factor, stage),
            shapes,
            scratch,
            3 * 1024 * 3072 * 256 * (2 if stage == 2 else 1),
            *operands,
            plan=plan,
            aliases=aliases,
        )

    def pack(half, keep, got, *packed):
        return call(
            functools.partial(pack_kernel, half),
            jax.ShapeDtypeStruct((8, height, ROWS), i16),
            [pltpu.VMEM((ROWS, ROWS), f32), powers],
            1 << 20,
            keep,
            got,
            *packed,
            plan=plan,
            aliases={3: 0} if packed else {},
        )

    keep, sums = score(0, (keep_shape, sums_shape), [], *near, *near_mate)
    *far, keep, sums = lax.optimization_barrier((*far, keep, sums))
    far_mate = [swap_core(piece) for piece in far]
    keep, _, send_near = score(
        1,
        (keep_shape, sums_shape, send_shape),
        [powers],
        *far,
        *near_mate,
        keep,
        sums,
        aliases={9: 0, 10: 1},
    )
    got_near = swap_core(send_near)
    keep, send_far = score(
        2,
        (keep_shape, send_shape),
        [powers, pltpu.VMEM((8, ROWS, ROWS), f32)],
        *near,
        *far,
        *far_mate,
        keep,
        aliases={13: 0},
    )
    got_far = swap_core(send_far)
    packed = pack(1, keep, got_far, pack(0, keep, got_near))
    one = jax.ShapeDtypeStruct((ROWS, ROWS), f32)
    keep, send = call(functools.partial(sum_kernel, factor), (one, one), [], 1 << 20, meet(packed))
    got = swap_core(send)
    return jnp.where(core == 0, keep, got), jnp.where(core == 0, got, keep)


def solution(mesh):
    fine = Mesh(mesh.devices.reshape(2, 2, 4, 4, 2), AXES)
    split = P(AXES, None)
    return jax.shard_map(
        shards,
        mesh=fine,
        in_specs=(split, split, P(AXES), P()),
        out_specs=(split, split),
        check_vma=False,
    )
```

```python
import functools
import math

import jax
import jax.numpy as jnp
from jax import lax
from jax.experimental import pallas as pl
from jax.experimental.pallas import tpu as pltpu
from jax.sharding import Mesh, PartitionSpec as P

logit_scale = 2.0
logit_bias = -6.0
AXES = ("xl", "core", "z", "y", "xh")
ROWS = 256
NOTE = 16
PEAK = 32000.0
VMEM = pl.BlockSpec(memory_space=pltpu.VMEM)
SMEM = pl.BlockSpec(memory_space=pltpu.SMEM)


def member(xl, core, z, y, xh):
    return (((xl * 2 + core) * 4 + z) * 4 + y) * 2 + xh


def teams():
    out = []
    for pair in ((0, 1), (2, 3)):
        for x in range(4):
            out.append([member(x % 2, 0, z, y, x // 2) for z in pair for y in range(4)])
    for pair in ((0, 3), (1, 2)):
        for y in range(4):
            out.append([member(x % 2, 1, z, y, x // 2) for z in pair for x in range(4)])
    return out


def step(value, level, shift):
    pairs = []
    for team in teams():
        for i in range(8):
            pairs.append((team[i], team[(i // 4 + level) % 2 * 4 + (i + shift) % 4]))
    return lax.ppermute(value, AXES, pairs)


def meet(value):
    return lax.all_to_all(value, AXES, 0, 0, axis_index_groups=teams(), tiled=True)


def swap_core(value):
    return lax.ppermute(value, "core", [(0, 1), (1, 0)])


def encode(block):
    top = jnp.maximum(jnp.max(jnp.abs(block), axis=0, keepdims=True), 2.0**-100)
    power = jnp.ceil(jnp.log2(top) * 128.0) + 1.0
    scaled = block * (PEAK * jnp.exp2(power * (-1.0 / 128.0)))
    return jnp.floor(scaled + 0.5).astype(jnp.int16), power


def decode(code, power):
    return code.astype(jnp.float32) * (jnp.exp2(power * (1.0 / 128.0)) * (1.0 / PEAK))


def notes(powers):
    powers = powers + [jnp.zeros((1, ROWS), jnp.float32)] * (NOTE - len(powers))
    return jnp.concatenate(powers, axis=0).astype(jnp.int16)


def on_core(body):
    core = lax.axis_index("core")
    for number in range(2):
        pl.when(core == number)(functools.partial(body, number))


def unused(plan):
    return plan[0, 0] ^ plan[1, 0]


def place(number, skip):
    return jnp.where(number == skip, 0, number - jnp.where(skip < number, 1, 0))


def build_kernel(own, ids, a_got, b_got, ids_got, out):
    def body(core):
        other = 1 - core
        out[core * ROWS : (core + 1) * ROWS, :] = own[...]
        out[other * ROWS : (other + 1) * ROWS, :] = (a_got if core == 0 else b_got)[...]
        rows = [ids[...].astype(jnp.float32), ids_got[...].astype(jnp.float32)]
        rows.append(jnp.zeros((NOTE - 4, ROWS), jnp.float32))
        out[2 * ROWS :, :] = jnp.concatenate(rows, axis=0).astype(jnp.bfloat16)

    on_core(body)


def score_kernel(factor, stage, plan, *refs):
    sets = [([0], [0]), ([1], [0]), ([0, 1], [1])][stage]
    mine = {which: refs[4 * i : 4 * i + 4] for i, which in enumerate(sets[0])}
    refs = refs[4 * len(sets[0]) :]
    theirs = {sets[1][0]: refs[:4]}
    if stage == 0:
        keep, sums = refs[4:]
        send = powers = None
    elif stage == 1:
        keep, sums, send, powers = refs[6:]
    else:
        keep, send, powers, sums = refs[5:]
    half_scale = 0.5 * factor
    half_bias = 0.5 * logit_bias
    wide, deep = 4 * ROWS, 2 * ROWS
    xl, xh = lax.axis_index("xl"), lax.axis_index("xh")
    z, y = lax.axis_index("z"), lax.axis_index("y")
    skip = unused(plan)

    def add(ref, start, value, fresh):
        count = value.shape[0] // ROWS
        value = value.reshape(count, ROWS, ROWS)
        if not fresh:
            value = value + ref[start : start + count]
        ref[start : start + count] = value

    def body(core):
        first, second = (mine, theirs) if core == 0 else (theirs, mine)
        for a_set, a_pieces in first.items():
            ids = []
            for piece in a_pieces:
                note = piece[2 * ROWS :, :].astype(jnp.float32)[2 * core : 2 * core + 2]
                ids.append((note[0:1] * 256.0 + note[1:2]).astype(jnp.int32))
            ids = jnp.concatenate(ids, axis=1)
            for b_set, b_pieces in second.items():
                for number in range(4):
                    side = core ^ (number & 1)
                    offsets = (number // 2, number // 2 + 2)

                    def tile(number=number, side=side, offsets=offsets, a_pieces=a_pieces, ids=ids, a_set=a_set, b_set=b_set, b_pieces=b_pieces):
                        a = [piece[core * ROWS : (core + 1) * ROWS, :] for piece in a_pieces]
                        a = jnp.concatenate(a, axis=0)
                        keys = [b_pieces[o][side * ROWS : (side + 1) * ROWS, :] for o in offsets]
                        keys = jnp.concatenate(keys, axis=0)
                        rows = jnp.full_like(ids, -1)
                        for place_of, o in enumerate(offsets):
                            x = (xh * 2 + xl + o) % 4
                            level = 3 - z if b_set else z
                            base = (x % 2 * 2 + side) * 32 + level * 8 + y * 2 + x // 2
                            here = lax.shift_right_logical(ids, 8) == base
                            rows = jnp.where(here, (ids & 255) + place_of * ROWS, rows)
                        hit = lax.broadcasted_iota(jnp.int32, (deep, wide), 0) == rows
                        logits = lax.dot_general(
                            keys, a, (((1,), (1,)), ((), ())), preferred_element_type=jnp.float32
                        )
                        weights = 0.5 * jnp.tanh(logits * half_scale + half_bias)
                        weights = (weights + jnp.where(hit, -0.5, 0.5)).astype(jnp.bfloat16)
                        gb = jnp.dot(weights, a, preferred_element_type=jnp.float32)
                        ga = lax.dot_general(
                            weights, keys, (((0,), (0,)), ((), ())), preferred_element_type=jnp.float32
                        )
                        if core == 0:
                            add(sums, number * 2, gb, stage == 0 or (stage == 2 and a_set == 0))
                            add(keep, a_set * 4, ga, stage < 2 and number == 0)
                        else:
                            add(keep, b_set * 8 + number * 2, gb, stage < 2)
                            add(sums, 0, ga, number == 0 and (stage == 0 or (stage == 2 and b_set == 0)))

                    if number:
                        pl.when(skip != number)(tile)
                    else:
                        tile()
        if stage == 0:
            return
        powers[...] = jnp.zeros_like(powers)
        for i in range(8 if core == 0 else 4):

            def write(i=i):
                code, power = encode(sums[i])
                at = place(i // 2, skip) * 2 + i % 2 if core == 0 else i
                send[pl.ds(pl.multiple_of(at * ROWS, ROWS), ROWS), :] = code
                powers[pl.ds(at, 1), :] = power

            if core == 0 and i > 1:
                pl.when(skip != i // 2)(write)
            else:
                write()
        send[6 * ROWS :, :] = powers[...].astype(jnp.int16)

    on_core(body)


def pack_kernel(far, plan, keep, got, *refs):
    out, total, powers = refs[-3:]
    z, y = lax.axis_index("z"), lax.axis_index("y")
    x = lax.axis_index("xh") * 2 + lax.axis_index("xl")
    skip = unused(plan)

    def body(core):
        if core == 0:
            got_powers = got[6 * ROWS :, :].astype(jnp.float32)
            level, at = z % 2, y
        else:
            powers[...] = got[6 * ROWS :, :].astype(jnp.float32)
            level, at = z // 2, x
        if far:
            level = 1 - level
        for o in range(4):
            s = level * 4 + (at + o) % 4
            written = []
            if core == 0:
                code, power = encode(keep[far * 4 + o])
                out[s, 0:ROWS, :] = code
                out[s, ROWS : 2 * ROWS, :] = got[o * ROWS : (o + 1) * ROWS, :]
                written = [power, got_powers[o : o + 1]]
            else:
                for c in range(2):
                    number = o % 2 * 2 + (1 - c)
                    value = jnp.where(skip != number, keep[far * 8 + number * 2 + o // 2], 0.0)
                    number = number ^ 1
                    used = jnp.where(skip != number, 1.0 / PEAK, 0.0)
                    index = place(number, skip) * 2 + o // 2
                    scale = jnp.exp2(powers[pl.ds(index, 1), :] * (1.0 / 128.0)) * used
                    code = got[pl.ds(pl.multiple_of(index * ROWS, ROWS), ROWS), :]
                    total[...] = value + code.astype(jnp.float32) * scale
                    code, power = encode(total[...])
                    out[s, c * ROWS : (c + 1) * ROWS, :] = code
                    written.append(power)
            out[s, 2 * ROWS :, :] = notes(written)

    on_core(body)


def sum_kernel(factor, got, keep, send):
    def body(core):
        for c in range(2):
            total = jnp.zeros((ROWS, ROWS), jnp.float32)
            for s in range(8):
                power = got[s, 2 * ROWS :, :].astype(jnp.float32)[c : c + 1]
                total += decode(got[s, c * ROWS : (c + 1) * ROWS, :], power)
            (keep if c == core else send)[...] = total * factor

    on_core(body)


def call(kernel, shapes, scratch, flops, *operands, plan=None, aliases={}):
    operands = operands if plan is None else (plan, *operands)
    return pl.pallas_call(
        kernel,
        out_shape=shapes,
        in_specs=[VMEM if plan is None or i else SMEM for i in range(len(operands))],
        out_specs=jax.tree.map(lambda _: VMEM, shapes),
        scratch_shapes=scratch,
        input_output_aliases=aliases,
        compiler_params=pltpu.CompilerParams(vmem_limit_bytes=36 << 20),
        cost_estimate=pl.CostEstimate(flops=flops, bytes_accessed=8 << 20, transcendentals=0),
    )(*operands)


def shards(views_a, views_b, positives, plan):
    factor = logit_scale / math.sqrt(views_a.shape[1])
    f32, i16, bf16 = jnp.float32, jnp.int16, jnp.bfloat16
    height = 2 * ROWS + NOTE
    core = lax.axis_index("core")
    ids = jnp.stack([positives // 256, positives % 256]).astype(bf16)
    got = [swap_core(value) for value in (views_a, views_b, ids)]
    shared = jnp.where(core == 0, views_a, views_b)
    piece = jax.ShapeDtypeStruct((height, ROWS), bf16)
    own = call(build_kernel, piece, [], 1 << 10, shared, ids, *got)
    over = step(own, 1, 0)
    near = [step(own, 0, 4 - further) for further in range(1, 4)]
    *near, _ = lax.optimization_barrier((*near, over))
    near = [own, *near]
    far = [over] + [step(over, 0, 4 - further) for further in range(1, 4)]
    near_mate = [swap_core(piece) for piece in near]

    keep_shape = jax.ShapeDtypeStruct((16, ROWS, ROWS), f32)
    sums_shape = jax.ShapeDtypeStruct((8, ROWS, ROWS), f32)
    send_shape = jax.ShapeDtypeStruct((6 * ROWS + NOTE, ROWS), i16)
    powers = pltpu.VMEM((NOTE, ROWS), f32)

    def score(stage, shapes, scratch, *operands, aliases={}):
        return call(
            functools.partial(score_kernel, factor, stage),
            shapes,
            scratch,
            3 * 1024 * 3072 * 256 * (2 if stage == 2 else 1),
            *operands,
            plan=plan,
            aliases=aliases,
        )

    def pack(half, keep, got, *packed):
        return call(
            functools.partial(pack_kernel, half),
            jax.ShapeDtypeStruct((8, height, ROWS), i16),
            [pltpu.VMEM((ROWS, ROWS), f32), powers],
            1 << 20,
            keep,
            got,
            *packed,
            plan=plan,
            aliases={3: 0} if packed else {},
        )

    keep, sums = score(0, (keep_shape, sums_shape), [], *near, *near_mate)
    *far, keep, sums = lax.optimization_barrier((*far, keep, sums))
    far_mate = [swap_core(piece) for piece in far]
    keep, _, send_near = score(
        1,
        (keep_shape, sums_shape, send_shape),
        [powers],
        *far,
        *near_mate,
        keep,
        sums,
        aliases={9: 0, 10: 1},
    )
    got_near = swap_core(send_near)
    keep, send_far = score(
        2,
        (keep_shape, send_shape),
        [powers, pltpu.VMEM((8, ROWS, ROWS), f32)],
        *near,
        *far,
        *far_mate,
        keep,
        aliases={13: 0},
    )
    got_far = swap_core(send_far)
    packed = pack(1, keep, got_far, pack(0, keep, got_near))
    one = jax.ShapeDtypeStruct((ROWS, ROWS), f32)
    keep, send = call(functools.partial(sum_kernel, factor), (one, one), [], 1 << 20, meet(packed))
    got = swap_core(send)
    return jnp.where(core == 0, keep, got), jnp.where(core == 0, got, keep)


def solution(mesh):
    fine = Mesh(mesh.devices.reshape(2, 2, 4, 4, 2), AXES)
    split = P(AXES, None)
    return jax.shard_map(
        shards,
        mesh=fine,
        in_specs=(split, split, P(AXES), P()),
        out_specs=(split, split),
        check_vma=False,
    )
```

```python
import functools
import math

import jax
import jax.numpy as jnp
from jax import lax
from jax.experimental import pallas as pl
from jax.experimental.pallas import tpu as pltpu
from jax.sharding import Mesh, PartitionSpec as P

logit_scale = 2.0
logit_bias = -6.0
AXES = ("xl", "core", "z", "y", "xh")
ROWS = 256
NOTE = 16
PEAK = 32000.0
VMEM = pl.BlockSpec(memory_space=pltpu.VMEM)
SMEM = pl.BlockSpec(memory_space=pltpu.SMEM)


def member(xl, core, z, y, xh):
    return (((xl * 2 + core) * 4 + z) * 4 + y) * 2 + xh


def teams():
    out = []
    for pair in ((0, 1), (2, 3)):
        for x in range(4):
            out.append([member(x % 2, 0, z, y, x // 2) for z in pair for y in range(4)])
    for pair in ((0, 3), (1, 2)):
        for y in range(4):
            out.append([member(x % 2, 1, z, y, x // 2) for z in pair for x in range(4)])
    return out


def meet(value):
    return lax.all_to_all(value, AXES, 0, 0, axis_index_groups=teams(), tiled=True)


def swap_core(value):
    return lax.ppermute(value, "core", [(0, 1), (1, 0)])


def encode(block):
    top = jnp.maximum(jnp.max(jnp.abs(block), axis=0, keepdims=True), 2.0**-100)
    power = jnp.ceil(jnp.log2(top) * 128.0) + 1.0
    scaled = block * (PEAK * jnp.exp2(power * (-1.0 / 128.0)))
    return jnp.floor(scaled + 0.5).astype(jnp.int16), power


def decode(code, power):
    return code.astype(jnp.float32) * (jnp.exp2(power * (1.0 / 128.0)) * (1.0 / PEAK))


def notes(powers):
    powers = powers + [jnp.zeros((1, ROWS), jnp.float32)] * (NOTE - len(powers))
    return jnp.concatenate(powers, axis=0).astype(jnp.int16)


def on_core(body):
    core = lax.axis_index("core")
    for number in range(2):
        pl.when(core == number)(functools.partial(body, number))


def window(plan, core):
    group = lax.axis_index("xl") * 2 + core
    return [group, plan[0, group], plan[1, group]]


def place_in(owners, group):
    hits = [owner == group for owner in owners]
    used = jnp.logical_or(hits[0], jnp.logical_or(hits[1], hits[2]))
    return jnp.where(hits[1], 1, jnp.where(hits[2], 2, 0)), jnp.where(used, 1.0, 0.0)


def build_kernel(own, ids, a_got, b_got, ids_got, out):
    def body(core):
        one, two = (own, a_got) if core == 0 else (b_got, own)
        value = ids_got[...]
        rows = [ids[...].astype(jnp.float32)]
        rows.append(lax.shift_right_logical(value, 8).astype(jnp.float32))
        rows.append((value & 255).astype(jnp.float32))
        rows.append(jnp.zeros((NOTE - 4, ROWS), jnp.float32))
        note = jnp.concatenate(rows, axis=0).astype(jnp.bfloat16)
        for s in range(8):
            out[s, 0:ROWS, :] = one[...]
            out[s, ROWS : 2 * ROWS, :] = two[...]
            out[s, 2 * ROWS :, :] = note

    on_core(body)


def score_kernel(factor, half, plan, mine, theirs, *refs):
    keep, send, sums = refs[-3:]
    half_scale = 0.5 * factor
    half_bias = 0.5 * logit_bias
    wide, deep = 4 * ROWS, 2 * ROWS
    z, y = lax.axis_index("z"), lax.axis_index("y")
    outer = jnp.logical_or(z == 0, z == 3)

    def add(ref, start, value, fresh):
        count = value.shape[0] // ROWS
        value = value.reshape(count, ROWS, ROWS)
        if not fresh:
            value = value + ref[start : start + count]
        ref[start : start + count] = value

    def body(core):
        owners = window(plan, core)
        for unit in range(2):
            a_from, a_source = (mine, 4 * unit) if core == 0 else (theirs, 0)
            a = [a_from[a_source + s, core * ROWS : (core + 1) * ROWS, :] for s in range(4)]
            a = jnp.concatenate(a, axis=0)
            ids = []
            for s in range(4):
                note = a_from[a_source + s, 2 * ROWS :, :].astype(jnp.float32)[2 * core : 2 * core + 2]
                ids.append((note[0:1] * 256.0 + note[1:2]).astype(jnp.int32))
            ids = jnp.concatenate(ids, axis=1)
            far = half if core == 0 else unit
            level = jnp.where(outer, 3 * far, 1 + far)
            for slot in range(3):
                group = owners[slot]
                b_from, b_source = (theirs, 0) if core == 0 else (mine, 4 * unit)
                b_rows = pl.ds(pl.multiple_of(group % 2 * ROWS, ROWS), ROWS)
                keys = [b_from[b_source + 2 * xh + group // 2, b_rows, :] for xh in range(2)]
                keys = jnp.concatenate(keys, axis=0)
                here = lax.shift_right_logical(ids, 9) == group * 16 + level * 4 + y
                rows = jnp.where(here, ids & 511, -1)
                hit = lax.broadcasted_iota(jnp.int32, (deep, wide), 0) == rows
                logits = lax.dot_general(
                    keys, a, (((1,), (1,)), ((), ())), preferred_element_type=jnp.float32
                )
                weights = 0.5 * jnp.tanh(logits * half_scale + half_bias) + jnp.where(hit, -0.5, 0.5)
                weights = weights.astype(jnp.bfloat16)
                gb = jnp.dot(weights, a, preferred_element_type=jnp.float32)
                ga = lax.dot_general(
                    weights, keys, (((0,), (0,)), ((), ())), preferred_element_type=jnp.float32
                )
                if core == 0:
                    add(sums, slot * 2, gb, unit == 0)
                    add(keep, unit * 4, ga, half == 0 and slot == 0)
                else:
                    add(keep, slot * 4 + unit * 2, gb, half == 0)
                    add(sums, 0, ga, unit == 0 and slot == 0)
        powers = []
        for i in range(6 if core == 0 else 4):
            code, power = encode(sums[i])
            send[i * ROWS : (i + 1) * ROWS, :] = code
            powers.append(power)
        send[6 * ROWS :, :] = notes(powers)

    on_core(body)


def pack_kernel(half, plan, keep, got, *refs):
    out, total, powers = refs[-3:]

    def body(core):
        if core == 0:
            got_powers = got[6 * ROWS :, :].astype(jnp.float32)
        else:
            powers[...] = got[6 * ROWS :, :].astype(jnp.float32)
            own, mate = window(plan, 1), window(plan, 0)
        for i in range(4):
            s = half * 4 + i
            written = []
            if core == 0:
                code, power = encode(keep[s])
                out[s, 0:ROWS, :] = code
                out[s, ROWS : 2 * ROWS, :] = got[i * ROWS : (i + 1) * ROWS, :]
                written = [power, got_powers[i : i + 1]]
            else:
                for c in range(2):
                    group, xh = i % 2 * 2 + c, i // 2
                    slot, kept = place_in(own, group)
                    value = keep[slot * 4 + half * 2 + xh] * kept
                    slot, used = place_in(mate, group)
                    index = slot * 2 + xh
                    scale = jnp.exp2(powers[pl.ds(index, 1), :] * (1.0 / 128.0)) * (used * (1.0 / PEAK))
                    code = got[pl.ds(pl.multiple_of(index * ROWS, ROWS), ROWS), :]
                    total[...] = value + code.astype(jnp.float32) * scale
                    code, power = encode(total[...])
                    out[s, c * ROWS : (c + 1) * ROWS, :] = code
                    written.append(power)
            out[s, 2 * ROWS :, :] = notes(written)

    on_core(body)


def sum_kernel(factor, got, keep, send):
    def body(core):
        for c in range(2):
            total = jnp.zeros((ROWS, ROWS), jnp.float32)
            for s in range(8):
                power = got[s, 2 * ROWS :, :].astype(jnp.float32)[c : c + 1]
                total += decode(got[s, c * ROWS : (c + 1) * ROWS, :], power)
            (keep if c == core else send)[...] = total * factor

    on_core(body)


def call(kernel, shapes, scratch, flops, *operands, plan=None, aliases={}):
    operands = operands if plan is None else (plan, *operands)
    return pl.pallas_call(
        kernel,
        out_shape=shapes,
        in_specs=[VMEM if plan is None or i else SMEM for i in range(len(operands))],
        out_specs=jax.tree.map(lambda _: VMEM, shapes),
        scratch_shapes=scratch,
        input_output_aliases=aliases,
        compiler_params=pltpu.CompilerParams(vmem_limit_bytes=36 << 20),
        cost_estimate=pl.CostEstimate(flops=flops, bytes_accessed=8 << 20, transcendentals=0),
    )(*operands)


def shards(views_a, views_b, positives, plan):
    factor = logit_scale / math.sqrt(views_a.shape[1])
    f32, i16, bf16 = jnp.float32, jnp.int16, jnp.bfloat16
    height = 2 * ROWS + NOTE
    core = lax.axis_index("core")
    ids = positives.reshape(1, ROWS)
    got = [swap_core(value) for value in (views_a, views_b, ids)]
    own = jnp.where(core == 0, views_a, views_b)
    own_ids = jnp.stack([positives // 256, positives % 256]).astype(bf16)
    built = jax.ShapeDtypeStruct((8, height, ROWS), bf16)
    mine = meet(call(build_kernel, built, [], 1 << 10, own, own_ids, *got))
    near, far = swap_core(mine[:4]), swap_core(mine[4:])

    def score(half, theirs, *keep):
        return call(
            functools.partial(score_kernel, factor, half),
            (
                jax.ShapeDtypeStruct((12, ROWS, ROWS), f32),
                jax.ShapeDtypeStruct((6 * ROWS + NOTE, ROWS), i16),
            ),
            [pltpu.VMEM((6, ROWS, ROWS), f32)],
            3 * 2048 * 3072 * 256,
            mine,
            theirs,
            *keep,
            plan=plan,
            aliases={3: 0} if keep else {},
        )

    def pack(half, keep, got, *packed):
        return call(
            functools.partial(pack_kernel, half),
            jax.ShapeDtypeStruct((8, height, ROWS), i16),
            [pltpu.VMEM((ROWS, ROWS), f32), pltpu.VMEM((NOTE, ROWS), f32)],
            1 << 20,
            keep,
            got,
            *packed,
            plan=plan,
            aliases={3: 0} if packed else {},
        )

    keep, send_near = score(0, near)
    got_near = swap_core(send_near)
    keep, send_far = score(1, far, keep)
    got_far = swap_core(send_far)
    packed = pack(1, keep, got_far, pack(0, keep, got_near))
    one = jax.ShapeDtypeStruct((ROWS, ROWS), f32)
    keep, send = call(functools.partial(sum_kernel, factor), (one, one), [], 1 << 20, meet(packed))
    got = swap_core(send)
    return jnp.where(core == 0, keep, got), jnp.where(core == 0, got, keep)


def solution(mesh):
    fine = Mesh(mesh.devices.reshape(2, 2, 4, 4, 2), AXES)
    split = P(AXES, None)
    return jax.shard_map(
        shards,
        mesh=fine,
        in_specs=(split, split, P(AXES), P()),
        out_specs=(split, split),
        check_vma=False,
    )
```

```python
import functools
import math

import jax
import jax.numpy as jnp
from jax import lax
from jax.experimental import pallas as pl
from jax.experimental.pallas import tpu as pltpu
from jax.sharding import Mesh, PartitionSpec as P

logit_scale = 2.0
logit_bias = -6.0
AXES = ("xl", "core", "z", "y", "xh")
ROWS = 256
NOTE = 16
PEAK = 32000.0
VMEM = pl.BlockSpec(memory_space=pltpu.VMEM)
SMEM = pl.BlockSpec(memory_space=pltpu.SMEM)


def member(xl, core, z, y, xh):
    return (((xl * 2 + core) * 4 + z) * 4 + y) * 2 + xh


def teams():
    out = []
    for pair in ((0, 1), (2, 3)):
        for x in range(4):
            out.append([member(x % 2, 0, z, y, x // 2) for z in pair for y in range(4)])
    for pair in ((0, 3), (1, 2)):
        for y in range(4):
            out.append([member(x % 2, 1, z, y, x // 2) for z in pair for x in range(4)])
    return out


def meet(value):
    return lax.all_to_all(value, AXES, 0, 0, axis_index_groups=teams(), tiled=True)


def swap_core(value):
    return lax.ppermute(value, "core", [(0, 1), (1, 0)])


def encode(out, start, load):
    powers = []
    for first in range(0, ROWS, 128):
        block = load(first, first + 128)
        top = jnp.maximum(jnp.max(jnp.abs(block), axis=0, keepdims=True), 2.0**-100)
        power = jnp.ceil(jnp.log2(top) * 128.0) + 1.0
        scaled = block * (PEAK * jnp.exp2(power * (-1.0 / 128.0)))
        out[start : start + ROWS, first : first + 128] = scaled.astype(jnp.int16)
        powers.append(power)
    return jnp.concatenate(powers, axis=1)


def decode(code, power):
    return code.astype(jnp.float32) * (jnp.exp2(power * (1.0 / 128.0)) * (1.0 / PEAK))


def notes(powers):
    powers = powers + [jnp.zeros((1, ROWS), jnp.float32)] * (NOTE - len(powers))
    return jnp.concatenate(powers, axis=0).astype(jnp.int16)


def on_core(body):
    core = lax.axis_index("core")
    for number in range(2):
        pl.when(core == number)(functools.partial(body, number))


def window(plan, core):
    group = lax.axis_index("xl") * 2 + core
    return [group, plan[0, group], plan[1, group]]


def place_in(owners, group):
    hits = [owner == group for owner in owners]
    used = jnp.logical_or(hits[0], jnp.logical_or(hits[1], hits[2]))
    return jnp.where(hits[1], 1, jnp.where(hits[2], 2, 0)), jnp.where(used, 1.0, 0.0)


def build_kernel(own, ids, a_got, b_got, ids_got, out):
    def body(core):
        one, two = (own, a_got) if core == 0 else (b_got, own)
        value = ids_got[...]
        rows = [ids[...].astype(jnp.float32)]
        rows.append(lax.shift_right_logical(value, 8).astype(jnp.float32))
        rows.append((value & 255).astype(jnp.float32))
        rows.append(jnp.zeros((NOTE - 4, ROWS), jnp.float32))
        note = jnp.concatenate(rows, axis=0).astype(jnp.bfloat16)
        for s in range(8):
            out[s, 0:ROWS, :] = one[...]
            out[s, ROWS : 2 * ROWS, :] = two[...]
            out[s, 2 * ROWS :, :] = note

    on_core(body)


def score_kernel(factor, half, plan, mine, theirs, *refs):
    keep, send, sums = refs[-3:]
    half_scale = jnp.bfloat16(0.5 * factor)
    half_bias = 0.5 * logit_bias
    wide, deep = 4 * ROWS, 2 * ROWS
    z, y = lax.axis_index("z"), lax.axis_index("y")
    outer = jnp.logical_or(z == 0, z == 3)

    def add(ref, start, value, fresh):
        count = value.shape[0] // ROWS
        value = value.reshape(count, ROWS, ROWS)
        if not fresh:
            value = value + ref[start : start + count]
        ref[start : start + count] = value

    def body(core):
        owners = window(plan, core)
        for unit in range(2):
            a_from, a_source = (mine, 4 * unit) if core == 0 else (theirs, 0)
            a = [a_from[a_source + s, core * ROWS : (core + 1) * ROWS, :] for s in range(4)]
            a = jnp.concatenate(a, axis=0)
            ids = []
            for s in range(4):
                note = a_from[a_source + s, 2 * ROWS :, :].astype(jnp.float32)[2 * core : 2 * core + 2]
                ids.append((note[0:1] * 256.0 + note[1:2]).astype(jnp.int32))
            ids = jnp.concatenate(ids, axis=1)
            far = half if core == 0 else unit
            level = jnp.where(outer, 3 * far, 1 + far)
            for slot in range(3):
                group = owners[slot]
                b_from, b_source = (theirs, 0) if core == 0 else (mine, 4 * unit)
                b_rows = pl.ds(pl.multiple_of(group % 2 * ROWS, ROWS), ROWS)
                keys = [b_from[b_source + 2 * xh + group // 2, b_rows, :] for xh in range(2)]
                keys = jnp.concatenate(keys, axis=0)
                here = lax.shift_right_logical(ids, 9) == group * 16 + level * 4 + y
                rows = jnp.where(here, ids & 511, -1)
                hit = lax.broadcasted_iota(jnp.int32, (deep, wide), 0) == rows
                logits = lax.dot_general(
                    keys * half_scale, a, (((1,), (1,)), ((), ())), preferred_element_type=jnp.float32
                )
                weights = jnp.tanh(logits + half_bias) + jnp.where(hit, -1.0, 1.0)
                weights = weights.astype(jnp.bfloat16)
                gb = jnp.dot(weights, a, preferred_element_type=jnp.float32)
                ga = lax.dot_general(
                    weights, keys, (((0,), (0,)), ((), ())), preferred_element_type=jnp.float32
                )
                if core == 0:
                    add(sums, slot * 2, gb, unit == 0)
                    add(keep, unit * 4, ga, half == 0 and slot == 0)
                else:
                    add(keep, slot * 4 + unit * 2, gb, half == 0)
                    add(sums, 0, ga, unit == 0 and slot == 0)
        powers = []
        for i in range(6 if core == 0 else 4):
            powers.append(encode(send, i * ROWS, lambda first, last: sums[i, :, first:last]))
        send[6 * ROWS :, :] = notes(powers)

    on_core(body)


def pack_kernel(half, plan, keep, got, *refs):
    out, powers = refs[-2:]

    def body(core):
        if core == 0:
            got_powers = got[6 * ROWS :, :].astype(jnp.float32)
        else:
            powers[...] = got[6 * ROWS :, :].astype(jnp.float32)
            own, mate = window(plan, 1), window(plan, 0)
        for i in range(4):
            s = half * 4 + i
            written = []
            if core == 0:
                power = encode(out.at[s], 0, lambda first, last: keep[s, :, first:last])
                out[s, ROWS : 2 * ROWS, :] = got[i * ROWS : (i + 1) * ROWS, :]
                written = [power, got_powers[i : i + 1]]
            else:
                for c in range(2):
                    group, xh = i % 2 * 2 + c, i // 2
                    slot, kept = place_in(own, group)
                    block = slot * 4 + half * 2 + xh
                    slot, used = place_in(mate, group)
                    index = slot * 2 + xh
                    scale = jnp.exp2(powers[pl.ds(index, 1), :] * (1.0 / 128.0)) * (used * (1.0 / PEAK))
                    rows = pl.ds(pl.multiple_of(index * ROWS, ROWS), ROWS)

                    def load(first, last):
                        code = got[rows, first:last].astype(jnp.float32)
                        return keep[block, :, first:last] * kept + code * scale[:, first:last]

                    written.append(encode(out.at[s], c * ROWS, load))
            out[s, 2 * ROWS :, :] = notes(written)

    on_core(body)


def sum_kernel(factor, got, keep, send):
    def body(core):
        for c in range(2):
            total = jnp.zeros((ROWS, ROWS), jnp.float32)
            for s in range(8):
                power = got[s, 2 * ROWS :, :].astype(jnp.float32)[c : c + 1]
                total += decode(got[s, c * ROWS : (c + 1) * ROWS, :], power)
            (keep if c == core else send)[...] = total * factor

    on_core(body)


def call(kernel, shapes, scratch, flops, *operands, plan=None, aliases={}):
    operands = operands if plan is None else (plan, *operands)
    return pl.pallas_call(
        kernel,
        out_shape=shapes,
        in_specs=[VMEM if plan is None or i else SMEM for i in range(len(operands))],
        out_specs=jax.tree.map(lambda _: VMEM, shapes),
        scratch_shapes=scratch,
        input_output_aliases=aliases,
        compiler_params=pltpu.CompilerParams(vmem_limit_bytes=36 << 20),
        cost_estimate=pl.CostEstimate(flops=flops, bytes_accessed=8 << 20, transcendentals=0),
    )(*operands)


def shards(views_a, views_b, positives, plan):
    factor = logit_scale / math.sqrt(views_a.shape[1])
    f32, i16, bf16 = jnp.float32, jnp.int16, jnp.bfloat16
    height = 2 * ROWS + NOTE
    core = lax.axis_index("core")
    ids = positives.reshape(1, ROWS)
    got = [swap_core(value) for value in (views_a, views_b, ids)]
    own = jnp.where(core == 0, views_a, views_b)
    own_ids = jnp.stack([positives // 256, positives % 256]).astype(bf16)
    built = jax.ShapeDtypeStruct((8, height, ROWS), bf16)
    mine = meet(call(build_kernel, built, [], 1 << 10, own, own_ids, *got))
    near, far = swap_core(mine[:4]), swap_core(mine[4:])

    def score(half, theirs, *keep):
        return call(
            functools.partial(score_kernel, factor, half),
            (
                jax.ShapeDtypeStruct((12, ROWS, ROWS), f32),
                jax.ShapeDtypeStruct((6 * ROWS + NOTE, ROWS), i16),
            ),
            [pltpu.VMEM((6, ROWS, ROWS), f32)],
            3 * 2048 * 3072 * 256,
            mine,
            theirs,
            *keep,
            plan=plan,
            aliases={3: 0} if keep else {},
        )

    def pack(half, keep, got, *packed):
        return call(
            functools.partial(pack_kernel, half),
            jax.ShapeDtypeStruct((8, height, ROWS), i16),
            [pltpu.VMEM((NOTE, ROWS), f32)],
            1 << 20,
            keep,
            got,
            *packed,
            plan=plan,
            aliases={3: 0} if packed else {},
        )

    keep, send_near = score(0, near)
    got_near = swap_core(send_near)
    keep, send_far = score(1, far, keep)
    got_far = swap_core(send_far)
    packed = pack(1, keep, got_far, pack(0, keep, got_near))
    one = jax.ShapeDtypeStruct((ROWS, ROWS), f32)
    keep, send = call(functools.partial(sum_kernel, 0.5 * factor), (one, one), [], 1 << 20, meet(packed))
    got = swap_core(send)
    return jnp.where(core == 0, keep, got), jnp.where(core == 0, got, keep)


def solution(mesh):
    fine = Mesh(mesh.devices.reshape(2, 2, 4, 4, 2), AXES)
    split = P(AXES, None)
    return jax.shard_map(
        shards,
        mesh=fine,
        in_specs=(split, split, P(AXES), P()),
        out_specs=(split, split),
        check_vma=False,
    )
```

```python
import functools
import math

import jax
import jax.numpy as jnp
from jax import lax
from jax.experimental import pallas as pl
from jax.experimental.pallas import tpu as pltpu
from jax.sharding import Mesh, PartitionSpec as P

logit_scale = 2.0
logit_bias = -6.0
AXES = ("xl", "core", "z", "y", "xh")
ROWS = 256
NOTE = 16
PEAK = 32000.0
VMEM = pl.BlockSpec(memory_space=pltpu.VMEM)
SMEM = pl.BlockSpec(memory_space=pltpu.SMEM)


def member(xl, core, z, y, xh):
    return (((xl * 2 + core) * 4 + z) * 4 + y) * 2 + xh


def teams():
    out = []
    for pair in ((0, 1), (2, 3)):
        for x in range(4):
            out.append([member(x % 2, 0, z, y, x // 2) for z in pair for y in range(4)])
    for pair in ((0, 3), (1, 2)):
        for y in range(4):
            out.append([member(x % 2, 1, z, y, x // 2) for z in pair for x in range(4)])
    return out


def meet(value):
    return lax.all_to_all(value, AXES, 0, 0, axis_index_groups=teams(), tiled=True)


def swap_core(value):
    return lax.ppermute(value, "core", [(0, 1), (1, 0)])


def encode(blocks):
    tops = [jnp.max(jnp.abs(load()), axis=0, keepdims=True) for load, _ in blocks]
    top = jnp.maximum(jnp.concatenate(tops, axis=0), 2.0**-100)
    power = jnp.ceil(jnp.log2(top) * 128.0) + 1.0
    scale = PEAK * jnp.exp2(power * (-1.0 / 128.0))
    for i, (load, store) in enumerate(blocks):
        store((load() * scale[i : i + 1]).astype(jnp.int16))
    return power


def decode(code, power):
    return code.astype(jnp.float32) * (jnp.exp2(power * (1.0 / 128.0)) * (1.0 / PEAK))


def notes(powers):
    powers = powers + [jnp.zeros((NOTE - sum(p.shape[0] for p in powers), ROWS), jnp.float32)]
    return jnp.concatenate(powers, axis=0).astype(jnp.int16)


def on_core(body):
    core = lax.axis_index("core")
    for number in range(2):
        pl.when(core == number)(functools.partial(body, number))


def window(plan, core):
    group = lax.axis_index("xl") * 2 + core
    return [group, plan[0, group], plan[1, group]]


def place_in(owners, group):
    hits = [owner == group for owner in owners]
    used = jnp.logical_or(hits[0], jnp.logical_or(hits[1], hits[2]))
    return jnp.where(hits[1], 1, jnp.where(hits[2], 2, 0)), jnp.where(used, 1.0, 0.0)


def build_kernel(own, ids, a_got, b_got, ids_got, out):
    def body(core):
        one, two = (own, a_got) if core == 0 else (b_got, own)
        value = ids_got[...]
        rows = [ids[...].astype(jnp.float32)]
        rows.append(lax.shift_right_logical(value, 8).astype(jnp.float32))
        rows.append((value & 255).astype(jnp.float32))
        rows.append(jnp.zeros((NOTE - 4, ROWS), jnp.float32))
        note = jnp.concatenate(rows, axis=0).astype(jnp.bfloat16)
        for s in range(8):
            out[s, 0:ROWS, :] = one[...]
            out[s, ROWS : 2 * ROWS, :] = two[...]
            out[s, 2 * ROWS :, :] = note

    on_core(body)


def score_kernel(factor, half, plan, mine, theirs, *refs):
    keep, send, sums = refs[-3:]
    half_scale = jnp.bfloat16(0.5 * factor)
    half_bias = 0.5 * logit_bias
    wide, deep = 4 * ROWS, 2 * ROWS
    z, y = lax.axis_index("z"), lax.axis_index("y")
    outer = jnp.logical_or(z == 0, z == 3)

    def add(ref, start, value, fresh):
        count = value.shape[0] // ROWS
        value = value.reshape(count, ROWS, ROWS)
        if not fresh:
            value = value + ref[start : start + count]
        ref[start : start + count] = value

    def body(core):
        owners = window(plan, core)
        for unit in range(2):
            a_from, a_source = (mine, 4 * unit) if core == 0 else (theirs, 0)
            a = [a_from[a_source + s, core * ROWS : (core + 1) * ROWS, :] for s in range(4)]
            a = jnp.concatenate(a, axis=0)
            ids = []
            for s in range(4):
                note = a_from[a_source + s, 2 * ROWS :, :].astype(jnp.float32)[2 * core : 2 * core + 2]
                ids.append((note[0:1] * 256.0 + note[1:2]).astype(jnp.int32))
            ids = jnp.concatenate(ids, axis=1)
            far = half if core == 0 else unit
            level = jnp.where(outer, 3 * far, 1 + far)
            for slot in range(3):
                group = owners[slot]
                b_from, b_source = (theirs, 0) if core == 0 else (mine, 4 * unit)
                b_rows = pl.ds(pl.multiple_of(group % 2 * ROWS, ROWS), ROWS)
                keys = [b_from[b_source + 2 * xh + group // 2, b_rows, :] for xh in range(2)]
                keys = jnp.concatenate(keys, axis=0)
                here = lax.shift_right_logical(ids, 9) == group * 16 + level * 4 + y
                rows = jnp.where(here, ids & 511, -1)
                hit = lax.broadcasted_iota(jnp.int32, (deep, wide), 0) == rows
                logits = lax.dot_general(
                    keys * half_scale, a, (((1,), (1,)), ((), ())), preferred_element_type=jnp.float32
                )
                weights = jnp.tanh(logits + half_bias) + jnp.where(hit, -1.0, 1.0)
                weights = weights.astype(jnp.bfloat16)
                gb = jnp.dot(weights, a, preferred_element_type=jnp.float32)
                ga = lax.dot_general(
                    weights, keys, (((0,), (0,)), ((), ())), preferred_element_type=jnp.float32
                )
                if core == 0:
                    add(sums, slot * 2, gb, unit == 0)
                    add(keep, unit * 4, ga, half == 0 and slot == 0)
                else:
                    add(keep, slot * 4 + unit * 2, gb, half == 0)
                    add(sums, 0, ga, unit == 0 and slot == 0)

        def block(i):
            def store(code):
                send[i * ROWS : (i + 1) * ROWS, :] = code

            return lambda: sums[i], store

        power = encode([block(i) for i in range(6 if core == 0 else 4)])
        send[6 * ROWS :, :] = notes([power])

    on_core(body)


def pack_kernel(half, plan, keep, got, *refs):
    out, scales = refs[-2:]

    def body(core):
        got_powers = got[6 * ROWS :, :].astype(jnp.float32)
        if core == 1:
            scales[...] = jnp.exp2(got_powers * (1.0 / 128.0)) * (1.0 / PEAK)
            own, mate = window(plan, 1), window(plan, 0)

        def kept_block(i):
            s = half * 4 + i

            def store(code):
                out[s, 0:ROWS, :] = code

            return lambda: keep[s], store

        def summed_block(i, c):
            group, xh = i % 2 * 2 + c, i // 2
            slot, kept = place_in(own, group)
            block = slot * 4 + half * 2 + xh
            slot, used = place_in(mate, group)
            index = slot * 2 + xh
            rows = pl.ds(pl.multiple_of(index * ROWS, ROWS), ROWS)

            def load():
                code = got[rows, :].astype(jnp.float32)
                return keep[block] * kept + code * (scales[pl.ds(index, 1), :] * used)

            def store(code):
                out[half * 4 + i, c * ROWS : (c + 1) * ROWS, :] = code

            return load, store

        if core == 0:
            power = encode([kept_block(i) for i in range(4)])
            for i in range(4):
                out[half * 4 + i, ROWS : 2 * ROWS, :] = got[i * ROWS : (i + 1) * ROWS, :]
                out[half * 4 + i, 2 * ROWS :, :] = notes([power[i : i + 1], got_powers[i : i + 1]])
        else:
            power = encode([summed_block(i, c) for i in range(4) for c in range(2)])
            for i in range(4):
                out[half * 4 + i, 2 * ROWS :, :] = notes([power[2 * i : 2 * i + 2]])

    on_core(body)


def sum_kernel(factor, got, keep, send):
    def body(core):
        for c in range(2):
            total = jnp.zeros((ROWS, ROWS), jnp.float32)
            for s in range(8):
                power = got[s, 2 * ROWS :, :].astype(jnp.float32)[c : c + 1]
                total += decode(got[s, c * ROWS : (c + 1) * ROWS, :], power)
            (keep if c == core else send)[...] = total * factor

    on_core(body)


def call(kernel, shapes, scratch, flops, *operands, plan=None, aliases={}):
    operands = operands if plan is None else (plan, *operands)
    return pl.pallas_call(
        kernel,
        out_shape=shapes,
        in_specs=[VMEM if plan is None or i else SMEM for i in range(len(operands))],
        out_specs=jax.tree.map(lambda _: VMEM, shapes),
        scratch_shapes=scratch,
        input_output_aliases=aliases,
        compiler_params=pltpu.CompilerParams(vmem_limit_bytes=36 << 20),
        cost_estimate=pl.CostEstimate(flops=flops, bytes_accessed=8 << 20, transcendentals=0),
    )(*operands)


def shards(views_a, views_b, positives, plan):
    factor = logit_scale / math.sqrt(views_a.shape[1])
    f32, i16, bf16 = jnp.float32, jnp.int16, jnp.bfloat16
    height = 2 * ROWS + NOTE
    core = lax.axis_index("core")
    ids = positives.reshape(1, ROWS)
    got = [swap_core(value) for value in (views_a, views_b, ids)]
    own = jnp.where(core == 0, views_a, views_b)
    own_ids = jnp.stack([positives // 256, positives % 256]).astype(bf16)
    built = jax.ShapeDtypeStruct((8, height, ROWS), bf16)
    mine = meet(call(build_kernel, built, [], 1 << 10, own, own_ids, *got))
    near, far = swap_core(mine[:4]), swap_core(mine[4:])

    def score(half, theirs, *keep):
        return call(
            functools.partial(score_kernel, factor, half),
            (
                jax.ShapeDtypeStruct((12, ROWS, ROWS), f32),
                jax.ShapeDtypeStruct((6 * ROWS + NOTE, ROWS), i16),
            ),
            [pltpu.VMEM((6, ROWS, ROWS), f32)],
            3 * 2048 * 3072 * 256,
            mine,
            theirs,
            *keep,
            plan=plan,
            aliases={3: 0} if keep else {},
        )

    def pack(half, keep, got, *packed):
        return call(
            functools.partial(pack_kernel, half),
            jax.ShapeDtypeStruct((8, height, ROWS), i16),
            [pltpu.VMEM((NOTE, ROWS), f32)],
            1 << 20,
            keep,
            got,
            *packed,
            plan=plan,
            aliases={3: 0} if packed else {},
        )

    keep, send_near = score(0, near)
    got_near = swap_core(send_near)
    keep, send_far = score(1, far, keep)
    got_far = swap_core(send_far)
    packed = pack(1, keep, got_far, pack(0, keep, got_near))
    one = jax.ShapeDtypeStruct((ROWS, ROWS), f32)
    keep, send = call(functools.partial(sum_kernel, 0.5 * factor), (one, one), [], 1 << 20, meet(packed))
    got = swap_core(send)
    return jnp.where(core == 0, keep, got), jnp.where(core == 0, got, keep)


def solution(mesh):
    fine = Mesh(mesh.devices.reshape(2, 2, 4, 4, 2), AXES)
    split = P(AXES, None)
    return jax.shard_map(
        shards,
        mesh=fine,
        in_specs=(split, split, P(AXES), P()),
        out_specs=(split, split),
        check_vma=False,
    )
```

```python
import functools
import math

import jax
import jax.numpy as jnp
from jax import lax
from jax.experimental import pallas as pl
from jax.experimental.pallas import tpu as pltpu
from jax.sharding import Mesh, PartitionSpec as P

logit_scale = 2.0
logit_bias = -6.0
AXES = ("xl", "core", "z", "y", "xh")
ROWS = 256
NOTE = 16
PEAK = 32000.0
VMEM = pl.BlockSpec(memory_space=pltpu.VMEM)


def member(xl, core, z, y, xh):
    return (((xl * 2 + core) * 4 + z) * 4 + y) * 2 + xh


def teams():
    out = []
    for pair in ((0, 1), (2, 3)):
        for x in range(4):
            out.append([member(x % 2, 0, z, y, x // 2) for z in pair for y in range(4)])
    for pair in ((0, 3), (1, 2)):
        for y in range(4):
            out.append([member(x % 2, 1, z, y, x // 2) for z in pair for x in range(4)])
    return out


def meet(value):
    return lax.all_to_all(value, AXES, 0, 0, axis_index_groups=teams(), tiled=True)


def swap_core(value):
    return lax.ppermute(value, "core", [(0, 1), (1, 0)])


def encode(out, start, load):
    powers = []
    for first in range(0, ROWS, 128):
        block = load(first, first + 128)
        top = jnp.maximum(jnp.max(jnp.abs(block), axis=0, keepdims=True), 2.0**-100)
        power = jnp.ceil(jnp.log2(top) * 128.0) + 1.0
        scaled = block * (PEAK * jnp.exp2(power * (-1.0 / 128.0)))
        out[start : start + ROWS, first : first + 128] = scaled.astype(jnp.int16)
        powers.append(power)
    return jnp.concatenate(powers, axis=1)


def decode(code, power):
    return code.astype(jnp.float32) * (jnp.exp2(power * (1.0 / 128.0)) * (1.0 / PEAK))


def notes(powers):
    powers = powers + [jnp.zeros((1, ROWS), jnp.float32)] * (NOTE - len(powers))
    return jnp.concatenate(powers, axis=0).astype(jnp.int16)


def on_core(body):
    core = lax.axis_index("core")
    for number in range(2):
        pl.when(core == number)(functools.partial(body, number))


def window(plan, core):
    group = lax.axis_index("xl") * 2 + core
    value = plan[...]
    return [group, group ^ value[0, 0], group ^ value[1, 0]]


def place_in(owners, group):
    hits = [owner == group for owner in owners]
    used = jnp.logical_or(hits[0], jnp.logical_or(hits[1], hits[2]))
    return jnp.where(hits[1], 1, jnp.where(hits[2], 2, 0)), jnp.where(used, 1.0, 0.0)


def build_kernel(own, ids, a_got, b_got, ids_got, out):
    def body(core):
        one, two = (own, a_got) if core == 0 else (b_got, own)
        value = ids_got[...]
        rows = [ids[...].astype(jnp.float32)]
        rows.append(lax.shift_right_logical(value, 8).astype(jnp.float32))
        rows.append((value & 255).astype(jnp.float32))
        rows.append(jnp.zeros((NOTE - 4, ROWS), jnp.float32))
        note = jnp.concatenate(rows, axis=0).astype(jnp.bfloat16)
        for s in range(8):
            out[s, 0:ROWS, :] = one[...]
            out[s, ROWS : 2 * ROWS, :] = two[...]
            out[s, 2 * ROWS :, :] = note

    on_core(body)


def score_kernel(factor, half, plan, mine, theirs, *refs):
    keep, send, sums = refs[-3:]
    half_scale = jnp.bfloat16(0.5 * factor)
    half_bias = 0.5 * logit_bias
    wide, deep = 4 * ROWS, 2 * ROWS
    z, y = lax.axis_index("z"), lax.axis_index("y")
    outer = jnp.logical_or(z == 0, z == 3)

    def add(ref, start, value, fresh):
        count = value.shape[0] // ROWS
        value = value.reshape(count, ROWS, ROWS)
        if not fresh:
            value = value + ref[start : start + count]
        ref[start : start + count] = value

    def body(core):
        owners = window(plan, core)
        for unit in range(2):
            a_from, a_source = (mine, 4 * unit) if core == 0 else (theirs, 0)
            a = [a_from[a_source + s, core * ROWS : (core + 1) * ROWS, :] for s in range(4)]
            a = jnp.concatenate(a, axis=0)
            ids = []
            for s in range(4):
                note = a_from[a_source + s, 2 * ROWS :, :].astype(jnp.float32)[2 * core : 2 * core + 2]
                ids.append((note[0:1] * 256.0 + note[1:2]).astype(jnp.int32))
            ids = jnp.concatenate(ids, axis=1)
            far = half if core == 0 else unit
            level = jnp.where(outer, 3 * far, 1 + far)
            for slot in range(3):
                group = owners[slot]
                b_from, b_source = (theirs, 0) if core == 0 else (mine, 4 * unit)
                b_rows = pl.ds(pl.multiple_of(group % 2 * ROWS, ROWS), ROWS)
                keys = [b_from[b_source + 2 * xh + group // 2, b_rows, :] for xh in range(2)]
                keys = jnp.concatenate(keys, axis=0)
                here = lax.shift_right_logical(ids, 9) == group * 16 + level * 4 + y
                rows = jnp.where(here, ids & 511, -1)
                hit = lax.broadcasted_iota(jnp.int32, (deep, wide), 0) == rows
                logits = lax.dot_general(
                    keys * half_scale, a, (((1,), (1,)), ((), ())), preferred_element_type=jnp.float32
                )
                weights = jnp.tanh(logits + half_bias) + jnp.where(hit, -1.0, 1.0)
                weights = weights.astype(jnp.bfloat16)
                gb = jnp.dot(weights, a, preferred_element_type=jnp.float32)
                ga = lax.dot_general(
                    weights, keys, (((0,), (0,)), ((), ())), preferred_element_type=jnp.float32
                )
                if core == 0:
                    add(sums, slot * 2, gb, unit == 0)
                    add(keep, unit * 4, ga, half == 0 and slot == 0)
                else:
                    add(keep, slot * 4 + unit * 2, gb, half == 0)
                    add(sums, 0, ga, unit == 0 and slot == 0)
        powers = []
        for i in range(6 if core == 0 else 4):
            powers.append(encode(send, i * ROWS, lambda first, last: sums[i, :, first:last]))
        send[6 * ROWS :, :] = notes(powers)

    on_core(body)


def pack_kernel(half, plan, keep, got, *refs):
    out, powers = refs[-2:]

    def body(core):
        if core == 0:
            got_powers = got[6 * ROWS :, :].astype(jnp.float32)
        else:
            powers[...] = got[6 * ROWS :, :].astype(jnp.float32)
            own, mate = window(plan, 1), window(plan, 0)
        for i in range(4):
            s = half * 4 + i
            written = []
            if core == 0:
                power = encode(out.at[s], 0, lambda first, last: keep[s, :, first:last])
                out[s, ROWS : 2 * ROWS, :] = got[i * ROWS : (i + 1) * ROWS, :]
                written = [power, got_powers[i : i + 1]]
            else:
                for c in range(2):
                    group, xh = i % 2 * 2 + c, i // 2
                    slot, kept = place_in(own, group)
                    block = slot * 4 + half * 2 + xh
                    slot, used = place_in(mate, group)
                    index = slot * 2 + xh
                    scale = jnp.exp2(powers[pl.ds(index, 1), :] * (1.0 / 128.0)) * (used * (1.0 / PEAK))
                    rows = pl.ds(pl.multiple_of(index * ROWS, ROWS), ROWS)

                    def load(first, last):
                        code = got[rows, first:last].astype(jnp.float32)
                        return keep[block, :, first:last] * kept + code * scale[:, first:last]

                    written.append(encode(out.at[s], c * ROWS, load))
            out[s, 2 * ROWS :, :] = notes(written)

    on_core(body)


def sum_kernel(factor, got, keep, send):
    def body(core):
        for c in range(2):
            total = jnp.zeros((ROWS, ROWS), jnp.float32)
            for s in range(8):
                power = got[s, 2 * ROWS :, :].astype(jnp.float32)[c : c + 1]
                total += decode(got[s, c * ROWS : (c + 1) * ROWS, :], power)
            (keep if c == core else send)[...] = total * factor

    on_core(body)


def call(kernel, shapes, scratch, flops, *operands, plan=None, aliases={}):
    operands = operands if plan is None else (plan, *operands)
    return pl.pallas_call(
        kernel,
        out_shape=shapes,
        in_specs=[VMEM] * len(operands),
        out_specs=jax.tree.map(lambda _: VMEM, shapes),
        scratch_shapes=scratch,
        input_output_aliases=aliases,
        compiler_params=pltpu.CompilerParams(vmem_limit_bytes=36 << 20),
        cost_estimate=pl.CostEstimate(flops=flops, bytes_accessed=8 << 20, transcendentals=0),
    )(*operands)


def shards(views_a, views_b, positives, plan):
    factor = logit_scale / math.sqrt(views_a.shape[1])
    f32, i16, bf16 = jnp.float32, jnp.int16, jnp.bfloat16
    height = 2 * ROWS + NOTE
    core = lax.axis_index("core")
    ids = positives.reshape(1, ROWS)
    got = [swap_core(value) for value in (views_a, views_b, ids)]
    own = jnp.where(core == 0, views_a, views_b)
    own_ids = jnp.stack([positives // 256, positives % 256]).astype(bf16)
    built = jax.ShapeDtypeStruct((8, height, ROWS), bf16)
    mine = meet(call(build_kernel, built, [], 1 << 10, own, own_ids, *got))
    near, far = swap_core(mine[:4]), swap_core(mine[4:])

    def score(half, theirs, *keep):
        return call(
            functools.partial(score_kernel, factor, half),
            (
                jax.ShapeDtypeStruct((12, ROWS, ROWS), f32),
                jax.ShapeDtypeStruct((6 * ROWS + NOTE, ROWS), i16),
            ),
            [pltpu.VMEM((6, ROWS, ROWS), f32)],
            3 * 2048 * 3072 * 256,
            mine,
            theirs,
            *keep,
            plan=plan,
            aliases={3: 0} if keep else {},
        )

    def pack(half, keep, got, *packed):
        return call(
            functools.partial(pack_kernel, half),
            jax.ShapeDtypeStruct((8, height, ROWS), i16),
            [pltpu.VMEM((NOTE, ROWS), f32)],
            1 << 20,
            keep,
            got,
            *packed,
            plan=plan,
            aliases={3: 0} if packed else {},
        )

    keep, send_near = score(0, near)
    got_near = swap_core(send_near)
    keep, send_far = score(1, far, keep)
    got_far = swap_core(send_far)
    packed = pack(1, keep, got_far, pack(0, keep, got_near))
    one = jax.ShapeDtypeStruct((ROWS, ROWS), f32)
    keep, send = call(functools.partial(sum_kernel, 0.5 * factor), (one, one), [], 1 << 20, meet(packed))
    got = swap_core(send)
    return jnp.where(core == 0, keep, got), jnp.where(core == 0, got, keep)


def solution(mesh):
    fine = Mesh(mesh.devices.reshape(2, 2, 4, 4, 2), AXES)
    split = P(AXES, None)
    return jax.shard_map(
        shards,
        mesh=fine,
        in_specs=(split, split, P(AXES), P()),
        out_specs=(split, split),
        check_vma=False,
    )
```

```python
import functools
import math

import jax
import jax.numpy as jnp
from jax import lax
from jax.experimental import pallas as pl
from jax.experimental.pallas import tpu as pltpu
from jax.sharding import Mesh, PartitionSpec as P

logit_scale = 2.0
logit_bias = -6.0
AXES = ("xl", "core", "z", "y", "xh")
ROWS = 256
NOTE = 16
PEAK = 32000.0
VMEM = pl.BlockSpec(memory_space=pltpu.VMEM)


def member(xl, core, z, y, xh):
    return (((xl * 2 + core) * 4 + z) * 4 + y) * 2 + xh


def teams():
    out = []
    for pair in ((0, 1), (2, 3)):
        for x in range(4):
            out.append([member(x % 2, 0, z, y, x // 2) for z in pair for y in range(4)])
    for pair in ((0, 3), (1, 2)):
        for y in range(4):
            out.append([member(x % 2, 1, z, y, x // 2) for z in pair for x in range(4)])
    return out


def meet(value):
    return lax.all_to_all(value, AXES, 0, 0, axis_index_groups=teams(), tiled=True)


def swap_core(value):
    return lax.ppermute(value, "core", [(0, 1), (1, 0)])


def encode(out, start, load):
    powers = []
    for first in range(0, ROWS, 128):
        block = load(first, first + 128)
        top = jnp.maximum(jnp.max(jnp.abs(block), axis=0, keepdims=True), 2.0**-100)
        power = jnp.ceil(jnp.log2(top) * 128.0) + 1.0
        scaled = block * (PEAK * jnp.exp2(power * (-1.0 / 128.0)))
        out[start : start + ROWS, first : first + 128] = scaled.astype(jnp.int16)
        powers.append(power)
    return jnp.concatenate(powers, axis=1)


def decode(code, power):
    return code.astype(jnp.float32) * (jnp.exp2(power * (1.0 / 128.0)) * (1.0 / PEAK))


def notes(powers):
    powers = powers + [jnp.zeros((1, ROWS), jnp.float32)] * (NOTE - len(powers))
    return jnp.concatenate(powers, axis=0).astype(jnp.int16)


def on_core(body):
    core = lax.axis_index("core")
    for number in range(2):
        pl.when(core == number)(functools.partial(body, number))


def window(plan, core):
    group = lax.axis_index("xl") * 2 + core
    value = plan[...]
    return [group, group ^ value[0, 0], group ^ value[1, 0]]


def place_in(owners, group):
    hits = [owner == group for owner in owners]
    used = jnp.logical_or(hits[0], jnp.logical_or(hits[1], hits[2]))
    return jnp.where(hits[1], 1, jnp.where(hits[2], 2, 0)), jnp.where(used, 1.0, 0.0)


def build_kernel(own, ids, a_got, b_got, ids_got, out):
    def body(core):
        one, two = (own, a_got) if core == 0 else (b_got, own)
        value = ids_got[...]
        rows = [ids[...].astype(jnp.float32)]
        rows.append(lax.shift_right_logical(value, 8).astype(jnp.float32))
        rows.append((value & 255).astype(jnp.float32))
        rows.append(jnp.zeros((NOTE - 4, ROWS), jnp.float32))
        note = jnp.concatenate(rows, axis=0).astype(jnp.bfloat16)
        for s in range(8):
            out[s, 0:ROWS, :] = one[...]
            out[s, ROWS : 2 * ROWS, :] = two[...]
            out[s, 2 * ROWS :, :] = note

    on_core(body)


def score_kernel(factor, half, plan, mine, theirs, *refs):
    keep, send, sums = refs[-3:]
    half_scale = jnp.bfloat16(0.5 * factor)
    half_bias = 0.5 * logit_bias
    z, y = lax.axis_index("z"), lax.axis_index("y")
    outer = jnp.logical_or(z == 0, z == 3)

    def add(ref, start, value, fresh):
        count = value.shape[0] // ROWS
        value = value.reshape(count, ROWS, ROWS)
        if not fresh:
            value = value + ref[start : start + count]
        ref[start : start + count] = value

    def body(core):
        owners = window(plan, core)
        a_from, b_from = (mine, theirs) if core == 0 else (theirs, mine)
        a = [a_from[s, core * ROWS : (core + 1) * ROWS, :] for s in range(a_from.shape[0])]
        a = jnp.concatenate(a, axis=0)
        ids = []
        for s in range(a_from.shape[0]):
            note = a_from[s, 2 * ROWS :, :].astype(jnp.float32)[2 * core : 2 * core + 2]
            ids.append((note[0:1] * 256.0 + note[1:2]).astype(jnp.int32))
        ids = jnp.concatenate(ids, axis=1)
        for slot in range(3):
            group = owners[slot]
            b_rows = pl.ds(pl.multiple_of(group % 2 * ROWS, ROWS), ROWS)
            keys, rows = [], jnp.full_like(ids, -1)
            for unit in range(b_from.shape[0] // 4):
                keys += [b_from[4 * unit + 2 * xh + group // 2, b_rows, :] for xh in range(2)]
                far = half if core == 0 else unit
                level = jnp.where(outer, 3 * far, 1 + far)
                here = lax.shift_right_logical(ids, 9) == group * 16 + level * 4 + y
                rows = jnp.where(here, (ids & 511) + unit * 512, rows)
            keys = jnp.concatenate(keys, axis=0)
            hit = lax.broadcasted_iota(jnp.int32, (keys.shape[0], a.shape[0]), 0) == rows
            logits = lax.dot_general(
                keys * half_scale, a, (((1,), (1,)), ((), ())), preferred_element_type=jnp.float32
            )
            weights = jnp.tanh(logits + half_bias) + jnp.where(hit, -1.0, 1.0)
            weights = weights.astype(jnp.bfloat16)
            gb = jnp.dot(weights, a, preferred_element_type=jnp.float32)
            ga = lax.dot_general(
                weights, keys, (((0,), (0,)), ((), ())), preferred_element_type=jnp.float32
            )
            if core == 0:
                add(sums, slot * 2, gb, True)
                add(keep, 0, ga, half == 0 and slot == 0)
            else:
                add(keep, slot * 4, gb, half == 0)
                add(sums, 0, ga, slot == 0)
        powers = []
        for i in range(6 if core == 0 else 4):
            powers.append(encode(send, i * ROWS, lambda first, last: sums[i, :, first:last]))
        send[6 * ROWS :, :] = notes(powers)

    on_core(body)


def pack_kernel(half, plan, keep, got, *refs):
    out, powers = refs[-2:]

    def body(core):
        if core == 0:
            got_powers = got[6 * ROWS :, :].astype(jnp.float32)
        else:
            powers[...] = got[6 * ROWS :, :].astype(jnp.float32)
            own, mate = window(plan, 1), window(plan, 0)
        for i in range(4):
            s = half * 4 + i
            written = []
            if core == 0:
                power = encode(out.at[s], 0, lambda first, last: keep[s, :, first:last])
                out[s, ROWS : 2 * ROWS, :] = got[i * ROWS : (i + 1) * ROWS, :]
                written = [power, got_powers[i : i + 1]]
            else:
                for c in range(2):
                    group, xh = i % 2 * 2 + c, i // 2
                    slot, kept = place_in(own, group)
                    block = slot * 4 + half * 2 + xh
                    slot, used = place_in(mate, group)
                    index = slot * 2 + xh
                    scale = jnp.exp2(powers[pl.ds(index, 1), :] * (1.0 / 128.0)) * (used * (1.0 / PEAK))
                    rows = pl.ds(pl.multiple_of(index * ROWS, ROWS), ROWS)

                    def load(first, last):
                        code = got[rows, first:last].astype(jnp.float32)
                        return keep[block, :, first:last] * kept + code * scale[:, first:last]

                    written.append(encode(out.at[s], c * ROWS, load))
            out[s, 2 * ROWS :, :] = notes(written)

    on_core(body)


def sum_kernel(factor, got, keep, send):
    def body(core):
        for c in range(2):
            total = jnp.zeros((ROWS, ROWS), jnp.float32)
            for s in range(8):
                power = got[s, 2 * ROWS :, :].astype(jnp.float32)[c : c + 1]
                total += decode(got[s, c * ROWS : (c + 1) * ROWS, :], power)
            (keep if c == core else send)[...] = total * factor

    on_core(body)


def call(kernel, shapes, scratch, flops, *operands, plan=None, aliases={}):
    operands = operands if plan is None else (plan, *operands)
    return pl.pallas_call(
        kernel,
        out_shape=shapes,
        in_specs=[VMEM] * len(operands),
        out_specs=jax.tree.map(lambda _: VMEM, shapes),
        scratch_shapes=scratch,
        input_output_aliases=aliases,
        compiler_params=pltpu.CompilerParams(vmem_limit_bytes=36 << 20),
        cost_estimate=pl.CostEstimate(flops=flops, bytes_accessed=8 << 20, transcendentals=0),
    )(*operands)


def shards(views_a, views_b, positives, plan):
    factor = logit_scale / math.sqrt(views_a.shape[1])
    f32, i16, bf16 = jnp.float32, jnp.int16, jnp.bfloat16
    height = 2 * ROWS + NOTE
    core = lax.axis_index("core")
    ids = positives.reshape(1, ROWS)
    got = [swap_core(value) for value in (views_a, views_b, ids)]
    own = jnp.where(core == 0, views_a, views_b)
    own_ids = jnp.stack([positives // 256, positives % 256]).astype(bf16)
    built = jax.ShapeDtypeStruct((8, height, ROWS), bf16)
    mine = meet(call(build_kernel, built, [], 1 << 10, own, own_ids, *got))
    near, far = swap_core(mine[:4]), swap_core(mine[4:])

    def score(half, theirs, *keep):
        return call(
            functools.partial(score_kernel, factor, half),
            (
                jax.ShapeDtypeStruct((12, ROWS, ROWS), f32),
                jax.ShapeDtypeStruct((6 * ROWS + NOTE, ROWS), i16),
            ),
            [pltpu.VMEM((6, ROWS, ROWS), f32)],
            3 * 2048 * 3072 * 256,
            mine,
            theirs,
            *keep,
            plan=plan,
            aliases={3: 0} if keep else {},
        )

    def pack(half, keep, got, *packed):
        return call(
            functools.partial(pack_kernel, half),
            jax.ShapeDtypeStruct((8, height, ROWS), i16),
            [pltpu.VMEM((NOTE, ROWS), f32)],
            1 << 20,
            keep,
            got,
            *packed,
            plan=plan,
            aliases={3: 0} if packed else {},
        )

    keep, send_near = score(0, near)
    got_near = swap_core(send_near)
    keep, send_far = score(1, far, keep)
    got_far = swap_core(send_far)
    packed = pack(1, keep, got_far, pack(0, keep, got_near))
    one = jax.ShapeDtypeStruct((ROWS, ROWS), f32)
    keep, send = call(functools.partial(sum_kernel, 0.5 * factor), (one, one), [], 1 << 20, meet(packed))
    got = swap_core(send)
    return jnp.where(core == 0, keep, got), jnp.where(core == 0, got, keep)


def solution(mesh):
    fine = Mesh(mesh.devices.reshape(2, 2, 4, 4, 2), AXES)
    split = P(AXES, None)
    return jax.shard_map(
        shards,
        mesh=fine,
        in_specs=(split, split, P(AXES), P()),
        out_specs=(split, split),
        check_vma=False,
    )
```

```python
import functools
import math

import jax
import jax.numpy as jnp
from jax import lax
from jax.experimental import pallas as pl
from jax.experimental.pallas import tpu as pltpu
from jax.sharding import Mesh, PartitionSpec as P

logit_scale = 2.0
logit_bias = -6.0
AXES = ("xl", "core", "z", "y", "xh")
ROWS = 256
NOTE = 16
PEAK = 32000.0
VMEM = pl.BlockSpec(memory_space=pltpu.VMEM)


def member(xl, core, z, y, xh):
    return (((xl * 2 + core) * 4 + z) * 4 + y) * 2 + xh


def teams():
    out = []
    for pair in ((0, 1), (2, 3)):
        for x in range(4):
            out.append([member(x % 2, 0, z, y, x // 2) for z in pair for y in range(4)])
    for pair in ((0, 3), (1, 2)):
        for y in range(4):
            out.append([member(x % 2, 1, z, y, x // 2) for z in pair for x in range(4)])
    return out


def meet(value):
    return lax.all_to_all(value, AXES, 0, 0, axis_index_groups=teams(), tiled=True)


def swap_core(value):
    return lax.ppermute(value, "core", [(0, 1), (1, 0)])


def encode(out, start, load):
    powers = []
    for first in range(0, ROWS, 128):
        block = load(first, first + 128)
        top = jnp.maximum(jnp.max(jnp.abs(block), axis=0, keepdims=True), 2.0**-100)
        power = jnp.ceil(jnp.log2(top) * 128.0) + 1.0
        scaled = block * (PEAK * jnp.exp2(power * (-1.0 / 128.0)))
        out[start : start + ROWS, first : first + 128] = scaled.astype(jnp.int16)
        powers.append(power)
    return jnp.concatenate(powers, axis=1)


def encode_all(out, blocks):
    tops = [jnp.max(jnp.abs(blocks[i]), axis=0, keepdims=True) for i in range(blocks.shape[0])]
    top = jnp.maximum(jnp.concatenate(tops, axis=0), 2.0**-100)
    power = jnp.ceil(jnp.log2(top) * 128.0) + 1.0
    scale = PEAK * jnp.exp2(power * (-1.0 / 128.0))
    for i in range(blocks.shape[0]):
        out[i * ROWS : (i + 1) * ROWS, :] = (blocks[i] * scale[i : i + 1]).astype(jnp.int16)
    return [power[i : i + 1] for i in range(blocks.shape[0])]


def decode(code, power):
    return code.astype(jnp.float32) * (jnp.exp2(power * (1.0 / 128.0)) * (1.0 / PEAK))


def notes(powers):
    powers = powers + [jnp.zeros((1, ROWS), jnp.float32)] * (NOTE - len(powers))
    return jnp.concatenate(powers, axis=0).astype(jnp.int16)


def on_core(body):
    core = lax.axis_index("core")
    for number in range(2):
        pl.when(core == number)(functools.partial(body, number))


def window(plan, core):
    group = lax.axis_index("xl") * 2 + core
    value = plan[...]
    return [group, group ^ value[0, 0], group ^ value[1, 0]]


def place_in(owners, group):
    hits = [owner == group for owner in owners]
    used = jnp.logical_or(hits[0], jnp.logical_or(hits[1], hits[2]))
    return jnp.where(hits[1], 1, jnp.where(hits[2], 2, 0)), jnp.where(used, 1.0, 0.0)


def build_kernel(own, ids, a_got, b_got, ids_got, out):
    def body(core):
        one, two = (own, a_got) if core == 0 else (b_got, own)
        value = ids_got[...]
        rows = [ids[...].astype(jnp.float32)]
        rows.append(lax.shift_right_logical(value, 8).astype(jnp.float32))
        rows.append((value & 255).astype(jnp.float32))
        rows.append(jnp.zeros((NOTE - 4, ROWS), jnp.float32))
        note = jnp.concatenate(rows, axis=0).astype(jnp.bfloat16)
        for s in range(8):
            out[s, 0:ROWS, :] = one[...]
            out[s, ROWS : 2 * ROWS, :] = two[...]
            out[s, 2 * ROWS :, :] = note

    on_core(body)


def score_kernel(factor, half, plan, mine, theirs, *refs):
    keep, send, sums = refs[-3:]
    half_scale = jnp.bfloat16(0.5 * factor)
    half_bias = 0.5 * logit_bias
    wide, deep = 4 * ROWS, 2 * ROWS
    z, y = lax.axis_index("z"), lax.axis_index("y")
    outer = jnp.logical_or(z == 0, z == 3)

    def add(ref, start, value, fresh):
        count = value.shape[0] // ROWS
        value = value.reshape(count, ROWS, ROWS)
        if not fresh:
            value = value + ref[start : start + count]
        ref[start : start + count] = value

    def body(core):
        owners = window(plan, core)
        for unit in range(2):
            a_from, a_source = (mine, 4 * unit) if core == 0 else (theirs, 0)
            a = [a_from[a_source + s, core * ROWS : (core + 1) * ROWS, :] for s in range(4)]
            a = jnp.concatenate(a, axis=0)
            ids = []
            for s in range(4):
                note = a_from[a_source + s, 2 * ROWS :, :].astype(jnp.float32)[2 * core : 2 * core + 2]
                ids.append((note[0:1] * 256.0 + note[1:2]).astype(jnp.int32))
            ids = jnp.concatenate(ids, axis=1)
            far = half if core == 0 else unit
            level = jnp.where(outer, 3 * far, 1 + far)
            for slot in range(3):
                group = owners[slot]
                b_from, b_source = (theirs, 0) if core == 0 else (mine, 4 * unit)
                b_rows = pl.ds(pl.multiple_of(group % 2 * ROWS, ROWS), ROWS)
                keys = [b_from[b_source + 2 * xh + group // 2, b_rows, :] for xh in range(2)]
                keys = jnp.concatenate(keys, axis=0)
                here = lax.shift_right_logical(ids, 9) == group * 16 + level * 4 + y
                rows = jnp.where(here, ids & 511, -1)
                hit = lax.broadcasted_iota(jnp.int32, (deep, wide), 0) == rows
                logits = lax.dot_general(
                    keys * half_scale, a, (((1,), (1,)), ((), ())), preferred_element_type=jnp.float32
                )
                weights = jnp.tanh(logits + half_bias) + jnp.where(hit, -1.0, 1.0)
                weights = weights.astype(jnp.bfloat16)
                gb = jnp.dot(weights, a, preferred_element_type=jnp.float32)
                ga = lax.dot_general(
                    weights, keys, (((0,), (0,)), ((), ())), preferred_element_type=jnp.float32
                )
                if core == 0:
                    add(sums, slot * 2, gb, unit == 0)
                    add(keep, unit * 4, ga, half == 0 and slot == 0)
                else:
                    add(keep, slot * 4 + unit * 2, gb, half == 0)
                    add(sums, 0, ga, unit == 0 and slot == 0)
        if core == 0:
            powers = encode_all(send, sums)
        else:
            powers = [
                encode(send, i * ROWS, lambda first, last: sums[i, :, first:last]) for i in range(4)
            ]
        send[6 * ROWS :, :] = notes(powers)

    on_core(body)


def pack_kernel(half, plan, keep, got, *refs):
    out, powers = refs[-2:]

    def body(core):
        if core == 0:
            got_powers = got[6 * ROWS :, :].astype(jnp.float32)
        else:
            powers[...] = got[6 * ROWS :, :].astype(jnp.float32)
            own, mate = window(plan, 1), window(plan, 0)
        for i in range(4):
            s = half * 4 + i
            written = []
            if core == 0:
                power = encode(out.at[s], 0, lambda first, last: keep[s, :, first:last])
                out[s, ROWS : 2 * ROWS, :] = got[i * ROWS : (i + 1) * ROWS, :]
                written = [power, got_powers[i : i + 1]]
            else:
                for c in range(2):
                    group, xh = i % 2 * 2 + c, i // 2
                    slot, kept = place_in(own, group)
                    block = slot * 4 + half * 2 + xh
                    slot, used = place_in(mate, group)
                    index = slot * 2 + xh
                    scale = jnp.exp2(powers[pl.ds(index, 1), :] * (1.0 / 128.0)) * (used * (1.0 / PEAK))
                    rows = pl.ds(pl.multiple_of(index * ROWS, ROWS), ROWS)

                    def load(first, last):
                        code = got[rows, first:last].astype(jnp.float32)
                        return keep[block, :, first:last] * kept + code * scale[:, first:last]

                    written.append(encode(out.at[s], c * ROWS, load))
            out[s, 2 * ROWS :, :] = notes(written)

    on_core(body)


def sum_kernel(factor, kept, got, out):
    def body(core):
        c = core if kept else 1 - core
        total = jnp.zeros((ROWS, ROWS), jnp.float32)
        for s in range(8):
            power = got[s, 2 * ROWS :, :].astype(jnp.float32)[c : c + 1]
            total += decode(got[s, c * ROWS : (c + 1) * ROWS, :], power)
        out[...] = total * factor

    on_core(body)


def call(kernel, shapes, scratch, flops, *operands, plan=None, aliases={}):
    operands = operands if plan is None else (plan, *operands)
    return pl.pallas_call(
        kernel,
        out_shape=shapes,
        in_specs=[VMEM] * len(operands),
        out_specs=jax.tree.map(lambda _: VMEM, shapes),
        scratch_shapes=scratch,
        input_output_aliases=aliases,
        compiler_params=pltpu.CompilerParams(vmem_limit_bytes=36 << 20),
        cost_estimate=pl.CostEstimate(flops=flops, bytes_accessed=8 << 20, transcendentals=0),
    )(*operands)


def shards(views_a, views_b, positives, plan):
    factor = logit_scale / math.sqrt(views_a.shape[1])
    f32, i16, bf16 = jnp.float32, jnp.int16, jnp.bfloat16
    height = 2 * ROWS + NOTE
    core = lax.axis_index("core")
    ids = positives.reshape(1, ROWS)
    got = [swap_core(value) for value in (views_a, views_b, ids)]
    own = jnp.where(core == 0, views_a, views_b)
    own_ids = jnp.stack([positives // 256, positives % 256]).astype(bf16)
    built = jax.ShapeDtypeStruct((8, height, ROWS), bf16)
    mine = meet(call(build_kernel, built, [], 1 << 10, own, own_ids, *got))
    near, far = swap_core(mine[:4]), swap_core(mine[4:])

    def score(half, theirs, *keep):
        return call(
            functools.partial(score_kernel, factor, half),
            (
                jax.ShapeDtypeStruct((12, ROWS, ROWS), f32),
                jax.ShapeDtypeStruct((6 * ROWS + NOTE, ROWS), i16),
            ),
            [pltpu.VMEM((6, ROWS, ROWS), f32)],
            3 * 2048 * 3072 * 256,
            mine,
            theirs,
            *keep,
            plan=plan,
            aliases={3: 0} if keep else {},
        )

    def pack(half, keep, got, *packed):
        return call(
            functools.partial(pack_kernel, half),
            jax.ShapeDtypeStruct((8, height, ROWS), i16),
            [pltpu.VMEM((NOTE, ROWS), f32)],
            1 << 20,
            keep,
            got,
            *packed,
            plan=plan,
            aliases={3: 0} if packed else {},
        )

    keep, send_near = score(0, near)
    got_near = swap_core(send_near)
    keep, send_far = score(1, far, keep)
    got_far = swap_core(send_far)
    packed = pack(1, keep, got_far, pack(0, keep, got_near))
    one = jax.ShapeDtypeStruct((ROWS, ROWS), f32)
    pieces = meet(packed)
    send, keep = [
        call(functools.partial(sum_kernel, 0.5 * factor, kept), one, [], 1 << 28, pieces)
        for kept in (False, True)
    ]
    got = swap_core(send)
    return jnp.where(core == 0, keep, got), jnp.where(core == 0, got, keep)


def solution(mesh):
    fine = Mesh(mesh.devices.reshape(2, 2, 4, 4, 2), AXES)
    split = P(AXES, None)
    return jax.shard_map(
        shards,
        mesh=fine,
        in_specs=(split, split, P(AXES), P()),
        out_specs=(split, split),
        check_vma=False,
    )
```

```python
import functools
import math

import jax
import jax.numpy as jnp
from jax import lax
from jax.experimental import pallas as pl
from jax.experimental.pallas import tpu as pltpu
from jax.sharding import Mesh, PartitionSpec as P

logit_scale = 2.0
logit_bias = -6.0
AXES = ("xl", "core", "z", "y", "xh")
ROWS = 256
NOTE = 16
PEAK = 32000.0
VMEM = pl.BlockSpec(memory_space=pltpu.VMEM)


def member(xl, core, z, y, xh):
    return (((xl * 2 + core) * 4 + z) * 4 + y) * 2 + xh


def teams():
    out = []
    for pair in ((0, 1), (2, 3)):
        for x in range(4):
            out.append([member(x % 2, 0, z, y, x // 2) for z in pair for y in range(4)])
    for pair in ((0, 3), (1, 2)):
        for y in range(4):
            out.append([member(x % 2, 1, z, y, x // 2) for z in pair for x in range(4)])
    return out


def meet(value):
    return lax.all_to_all(value, AXES, 0, 0, axis_index_groups=teams(), tiled=True)


def swap_core(value):
    return lax.ppermute(value, "core", [(0, 1), (1, 0)])


def encode(out, start, load):
    powers = []
    for first in range(0, ROWS, 128):
        block = load(first, first + 128)
        top = jnp.maximum(jnp.max(jnp.abs(block), axis=0, keepdims=True), 2.0**-100)
        power = jnp.ceil(jnp.log2(top) * 128.0) + 1.0
        scaled = block * (PEAK * jnp.exp2(power * (-1.0 / 128.0)))
        out[start : start + ROWS, first : first + 128] = scaled.astype(jnp.int16)
        powers.append(power)
    return jnp.concatenate(powers, axis=1)


def encode_all(out, blocks):
    tops = [jnp.max(jnp.abs(blocks[i]), axis=0, keepdims=True) for i in range(blocks.shape[0])]
    top = jnp.maximum(jnp.concatenate(tops, axis=0), 2.0**-100)
    power = jnp.ceil(jnp.log2(top) * 128.0) + 1.0
    scale = PEAK * jnp.exp2(power * (-1.0 / 128.0))
    for i in range(blocks.shape[0]):
        out[i * ROWS : (i + 1) * ROWS, :] = (blocks[i] * scale[i : i + 1]).astype(jnp.int16)
    return [power[i : i + 1] for i in range(blocks.shape[0])]


def decode(code, power):
    return code.astype(jnp.float32) * (jnp.exp2(power * (1.0 / 128.0)) * (1.0 / PEAK))


def notes(powers):
    powers = powers + [jnp.zeros((1, ROWS), jnp.float32)] * (NOTE - len(powers))
    return jnp.concatenate(powers, axis=0).astype(jnp.int16)


def on_core(body):
    core = lax.axis_index("core")
    for number in range(2):
        pl.when(core == number)(functools.partial(body, number))


def window(plan, core):
    group = lax.axis_index("xl") * 2 + core
    value = plan[...]
    return [group, group ^ value[0, 0], group ^ value[1, 0]]


def place_in(owners, group):
    hits = [owner == group for owner in owners]
    used = jnp.logical_or(hits[0], jnp.logical_or(hits[1], hits[2]))
    return jnp.where(hits[1], 1, jnp.where(hits[2], 2, 0)), jnp.where(used, 1.0, 0.0)


def build_kernel(own, ids, a_got, b_got, ids_got, out):
    def body(core):
        one, two = (own, a_got) if core == 0 else (b_got, own)
        value = ids_got[...]
        rows = [ids[...].astype(jnp.float32)]
        rows.append(lax.shift_right_logical(value, 8).astype(jnp.float32))
        rows.append((value & 255).astype(jnp.float32))
        rows.append(jnp.zeros((NOTE - 4, ROWS), jnp.float32))
        note = jnp.concatenate(rows, axis=0).astype(jnp.bfloat16)
        for s in range(8):
            out[s, 0:ROWS, :] = one[...]
            out[s, ROWS : 2 * ROWS, :] = two[...]
            out[s, 2 * ROWS :, :] = note

    on_core(body)


def pick_kernel(half, plan, mine, out):
    def body(core):
        if core == 0:
            for s in range(4):
                source = mine.at[half * 4 + s]
                out[s * ROWS : (s + 1) * ROWS, :] = source[ROWS : 2 * ROWS, :]
                start = 4 * ROWS + s * NOTE
                out[start : start + NOTE, :] = source[2 * ROWS :, :]
        else:
            owners = window(plan, 0)
            for slot in range(3):
                rows = pl.ds(pl.multiple_of(owners[slot] % 2 * ROWS, ROWS), ROWS)
                for xh in range(2):
                    start = (slot * 2 + xh) * ROWS
                    value = mine[half * 4 + 2 * xh + owners[slot] // 2, rows, :]
                    out[start : start + ROWS, :] = value

    on_core(body)


def score_kernel(factor, half, plan, mine, theirs, *refs):
    keep, send, sums = refs[-3:]
    half_scale = jnp.bfloat16(0.5 * factor)
    half_bias = 0.5 * logit_bias
    wide, deep = 4 * ROWS, 2 * ROWS
    z, y = lax.axis_index("z"), lax.axis_index("y")
    outer = jnp.logical_or(z == 0, z == 3)

    def add(ref, start, value, fresh):
        count = value.shape[0] // ROWS
        value = value.reshape(count, ROWS, ROWS)
        if not fresh:
            value = value + ref[start : start + count]
        ref[start : start + count] = value

    def body(core):
        owners = window(plan, core)
        for unit in range(2):
            if core == 0:
                a = [mine[4 * unit + s, 0:ROWS, :] for s in range(4)]
                tags = [mine[4 * unit + s, 2 * ROWS :, :] for s in range(4)]
            else:
                a = [theirs[s * ROWS : (s + 1) * ROWS, :] for s in range(4)]
                starts = [4 * ROWS + s * NOTE for s in range(4)]
                tags = [theirs[start : start + NOTE, :] for start in starts]
            a = jnp.concatenate(a, axis=0)
            ids = []
            for tag in tags:
                note = tag.astype(jnp.float32)[2 * core : 2 * core + 2]
                ids.append((note[0:1] * 256.0 + note[1:2]).astype(jnp.int32))
            ids = jnp.concatenate(ids, axis=1)
            far = half if core == 0 else unit
            level = jnp.where(outer, 3 * far, 1 + far)
            for slot in range(3):
                group = owners[slot]
                if core == 0:
                    keys = theirs[slot * 2 * ROWS : (slot + 1) * 2 * ROWS, :]
                else:
                    b_rows = pl.ds(pl.multiple_of(group % 2 * ROWS, ROWS), ROWS)
                    keys = [mine[4 * unit + 2 * xh + group // 2, b_rows, :] for xh in range(2)]
                    keys = jnp.concatenate(keys, axis=0)
                here = lax.shift_right_logical(ids, 9) == group * 16 + level * 4 + y
                rows = jnp.where(here, ids & 511, -1)
                hit = lax.broadcasted_iota(jnp.int32, (deep, wide), 0) == rows
                logits = lax.dot_general(
                    keys * half_scale, a, (((1,), (1,)), ((), ())), preferred_element_type=jnp.float32
                )
                weights = jnp.tanh(logits + half_bias) + jnp.where(hit, -1.0, 1.0)
                weights = weights.astype(jnp.bfloat16)
                gb = jnp.dot(weights, a, preferred_element_type=jnp.float32)
                ga = lax.dot_general(
                    weights, keys, (((0,), (0,)), ((), ())), preferred_element_type=jnp.float32
                )
                if core == 0:
                    add(sums, slot * 2, gb, unit == 0)
                    add(keep, unit * 4, ga, half == 0 and slot == 0)
                else:
                    add(keep, slot * 4 + unit * 2, gb, half == 0)
                    add(sums, 0, ga, unit == 0 and slot == 0)
        if core == 0:
            powers = encode_all(send, sums)
        else:
            powers = [
                encode(send, i * ROWS, lambda first, last: sums[i, :, first:last]) for i in range(4)
            ]
        send[6 * ROWS :, :] = notes(powers)

    on_core(body)


def pack_kernel(half, plan, keep, got, *refs):
    out, powers = refs[-2:]

    def body(core):
        if core == 0:
            got_powers = got[6 * ROWS :, :].astype(jnp.float32)
        else:
            powers[...] = got[6 * ROWS :, :].astype(jnp.float32)
            own, mate = window(plan, 1), window(plan, 0)
        for i in range(4):
            s = half * 4 + i
            written = []
            if core == 0:
                power = encode(out.at[s], 0, lambda first, last: keep[s, :, first:last])
                out[s, ROWS : 2 * ROWS, :] = got[i * ROWS : (i + 1) * ROWS, :]
                written = [power, got_powers[i : i + 1]]
            else:
                for c in range(2):
                    group, xh = i % 2 * 2 + c, i // 2
                    slot, kept = place_in(own, group)
                    block = slot * 4 + half * 2 + xh
                    slot, used = place_in(mate, group)
                    index = slot * 2 + xh
                    scale = jnp.exp2(powers[pl.ds(index, 1), :] * (1.0 / 128.0)) * (used * (1.0 / PEAK))
                    rows = pl.ds(pl.multiple_of(index * ROWS, ROWS), ROWS)

                    def load(first, last):
                        code = got[rows, first:last].astype(jnp.float32)
                        return keep[block, :, first:last] * kept + code * scale[:, first:last]

                    written.append(encode(out.at[s], c * ROWS, load))
            out[s, 2 * ROWS :, :] = notes(written)

    on_core(body)


def sum_kernel(factor, kept, got, out):
    def body(core):
        c = core if kept else 1 - core
        total = jnp.zeros((ROWS, ROWS), jnp.float32)
        for s in range(8):
            power = got[s, 2 * ROWS :, :].astype(jnp.float32)[c : c + 1]
            total += decode(got[s, c * ROWS : (c + 1) * ROWS, :], power)
        out[...] = total * factor

    on_core(body)


def call(kernel, shapes, scratch, flops, *operands, plan=None, aliases={}):
    operands = operands if plan is None else (plan, *operands)
    return pl.pallas_call(
        kernel,
        out_shape=shapes,
        in_specs=[VMEM] * len(operands),
        out_specs=jax.tree.map(lambda _: VMEM, shapes),
        scratch_shapes=scratch,
        input_output_aliases=aliases,
        compiler_params=pltpu.CompilerParams(vmem_limit_bytes=36 << 20),
        cost_estimate=pl.CostEstimate(flops=flops, bytes_accessed=8 << 20, transcendentals=0),
    )(*operands)


def shards(views_a, views_b, positives, plan):
    factor = logit_scale / math.sqrt(views_a.shape[1])
    f32, i16, bf16 = jnp.float32, jnp.int16, jnp.bfloat16
    height = 2 * ROWS + NOTE
    core = lax.axis_index("core")
    ids = positives.reshape(1, ROWS)
    got = [swap_core(value) for value in (views_a, views_b, ids)]
    own = jnp.where(core == 0, views_a, views_b)
    own_ids = jnp.stack([positives // 256, positives % 256]).astype(bf16)
    built = jax.ShapeDtypeStruct((8, height, ROWS), bf16)
    mine = meet(call(build_kernel, built, [], 1 << 10, own, own_ids, *got))
    picked = jax.ShapeDtypeStruct((6 * ROWS, ROWS), bf16)
    near, far = [
        swap_core(call(functools.partial(pick_kernel, half), picked, [], 1 << 10, mine, plan=plan))
        for half in range(2)
    ]

    def score(half, theirs, *keep):
        return call(
            functools.partial(score_kernel, factor, half),
            (
                jax.ShapeDtypeStruct((12, ROWS, ROWS), f32),
                jax.ShapeDtypeStruct((6 * ROWS + NOTE, ROWS), i16),
            ),
            [pltpu.VMEM((6, ROWS, ROWS), f32)],
            3 * 2048 * 3072 * 256,
            mine,
            theirs,
            *keep,
            plan=plan,
            aliases={3: 0} if keep else {},
        )

    def pack(half, keep, got, *packed):
        return call(
            functools.partial(pack_kernel, half),
            jax.ShapeDtypeStruct((8, height, ROWS), i16),
            [pltpu.VMEM((NOTE, ROWS), f32)],
            1 << 20,
            keep,
            got,
            *packed,
            plan=plan,
            aliases={3: 0} if packed else {},
        )

    keep, send_near = score(0, near)
    got_near = swap_core(send_near)
    keep, send_far = score(1, far, keep)
    got_far = swap_core(send_far)
    packed = pack(1, keep, got_far, pack(0, keep, got_near))
    one = jax.ShapeDtypeStruct((ROWS, ROWS), f32)
    pieces = meet(packed)
    send, keep = [
        call(functools.partial(sum_kernel, 0.5 * factor, kept), one, [], 1 << 28, pieces)
        for kept in (False, True)
    ]
    got = swap_core(send)
    return jnp.where(core == 0, keep, got), jnp.where(core == 0, got, keep)


def solution(mesh):
    fine = Mesh(mesh.devices.reshape(2, 2, 4, 4, 2), AXES)
    split = P(AXES, None)
    return jax.shard_map(
        shards,
        mesh=fine,
        in_specs=(split, split, P(AXES), P()),
        out_specs=(split, split),
        check_vma=False,
    )
```

```python
import functools
import math

import jax
import jax.numpy as jnp
from jax import lax
from jax.experimental import pallas as pl
from jax.experimental.pallas import tpu as pltpu
from jax.sharding import Mesh, PartitionSpec as P

logit_scale = 2.0
logit_bias = -6.0
AXES = ("xl", "core", "z", "y", "xh")
ROWS = 256
NOTE = 16
PEAK = 32000.0
VMEM = pl.BlockSpec(memory_space=pltpu.VMEM)


def member(xl, core, z, y, xh):
    return (((xl * 2 + core) * 4 + z) * 4 + y) * 2 + xh


def teams():
    out = []
    for pair in ((0, 1), (2, 3)):
        for x in range(4):
            out.append([member(x % 2, 0, z, y, x // 2) for z in pair for y in range(4)])
    for pair in ((0, 3), (1, 2)):
        for y in range(4):
            out.append([member(x % 2, 1, z, y, x // 2) for z in pair for x in range(4)])
    return out


def meet(value):
    return lax.all_to_all(value, AXES, 0, 0, axis_index_groups=teams(), tiled=True)


def swap_core(value):
    return lax.ppermute(value, "core", [(0, 1), (1, 0)])


def encode(out, start, load):
    powers = []
    for first in range(0, ROWS, 128):
        block = load(first, first + 128)
        top = jnp.maximum(jnp.max(jnp.abs(block), axis=0, keepdims=True), 2.0**-100)
        power = jnp.ceil(jnp.log2(top) * 128.0) + 1.0
        scaled = block * (PEAK * jnp.exp2(power * (-1.0 / 128.0)))
        out[start : start + ROWS, first : first + 128] = scaled.astype(jnp.int16)
        powers.append(power)
    return jnp.concatenate(powers, axis=1)


def encode_all(out, blocks):
    tops = [jnp.max(jnp.abs(blocks[i]), axis=0, keepdims=True) for i in range(blocks.shape[0])]
    top = jnp.maximum(jnp.concatenate(tops, axis=0), 2.0**-100)
    power = jnp.ceil(jnp.log2(top) * 128.0) + 1.0
    scale = PEAK * jnp.exp2(power * (-1.0 / 128.0))
    for i in range(blocks.shape[0]):
        out[i * ROWS : (i + 1) * ROWS, :] = (blocks[i] * scale[i : i + 1]).astype(jnp.int16)
    return [power[i : i + 1] for i in range(blocks.shape[0])]


def decode(code, power):
    return code.astype(jnp.float32) * (jnp.exp2(power * (1.0 / 128.0)) * (1.0 / PEAK))


def notes(powers):
    powers = powers + [jnp.zeros((1, ROWS), jnp.float32)] * (NOTE - len(powers))
    return jnp.concatenate(powers, axis=0).astype(jnp.int16)


def on_core(body):
    core = lax.axis_index("core")
    for number in range(2):
        pl.when(core == number)(functools.partial(body, number))


def window(plan, core):
    group = lax.axis_index("xl") * 2 + core
    value = plan[...]
    return [group, group ^ value[0, 0], group ^ value[1, 0]]


def place_in(owners, group):
    hits = [owner == group for owner in owners]
    used = jnp.logical_or(hits[0], jnp.logical_or(hits[1], hits[2]))
    return jnp.where(hits[1], 1, jnp.where(hits[2], 2, 0)), jnp.where(used, 1.0, 0.0)


def build_kernel(own, ids, a_got, b_got, ids_got, out):
    def body(core):
        one, two = (own, a_got) if core == 0 else (b_got, own)
        rows = []
        for ref in (ids, ids_got):
            value = ref[...]
            rows.append(lax.shift_right_logical(value, 8).astype(jnp.float32))
            rows.append((value & 255).astype(jnp.float32))
        rows.append(jnp.zeros((NOTE - 4, ROWS), jnp.float32))
        note = jnp.concatenate(rows, axis=0).astype(jnp.bfloat16)
        for s in range(8):
            out[s, 0:ROWS, :] = one[...]
            out[s, ROWS : 2 * ROWS, :] = two[...]
            out[s, 2 * ROWS :, :] = note

    on_core(body)


def pick_kernel(half, plan, mine, out):
    def body(core):
        if core == 0:
            for s in range(4):
                source = mine.at[half * 4 + s]
                out[s * ROWS : (s + 1) * ROWS, :] = source[ROWS : 2 * ROWS, :]
                start = 4 * ROWS + s * NOTE
                out[start : start + NOTE, :] = source[2 * ROWS :, :]
        else:
            owners = window(plan, 0)
            for slot in range(3):
                rows = pl.ds(pl.multiple_of(owners[slot] % 2 * ROWS, ROWS), ROWS)
                for xh in range(2):
                    start = (slot * 2 + xh) * ROWS
                    value = mine[half * 4 + 2 * xh + owners[slot] // 2, rows, :]
                    out[start : start + ROWS, :] = value

    on_core(body)


def score_kernel(factor, half, plan, mine, theirs, *refs):
    keep, send, sums = refs[-3:]
    half_scale = jnp.bfloat16(0.5 * factor)
    half_bias = 0.5 * logit_bias
    wide, deep = 4 * ROWS, 2 * ROWS
    z, y = lax.axis_index("z"), lax.axis_index("y")
    outer = jnp.logical_or(z == 0, z == 3)

    def add(ref, start, value, fresh):
        count = value.shape[0] // ROWS
        value = value.reshape(count, ROWS, ROWS)
        if not fresh:
            value = value + ref[start : start + count]
        ref[start : start + count] = value

    def body(core):
        owners = window(plan, core)
        for unit in range(2):
            if core == 0:
                a = [mine[4 * unit + s, 0:ROWS, :] for s in range(4)]
                tags = [mine[4 * unit + s, 2 * ROWS :, :] for s in range(4)]
            else:
                a = [theirs[s * ROWS : (s + 1) * ROWS, :] for s in range(4)]
                starts = [4 * ROWS + s * NOTE for s in range(4)]
                tags = [theirs[start : start + NOTE, :] for start in starts]
            a = jnp.concatenate(a, axis=0)
            ids = []
            for tag in tags:
                note = tag.astype(jnp.float32)[2 * core : 2 * core + 2]
                ids.append((note[0:1] * 256.0 + note[1:2]).astype(jnp.int32))
            ids = jnp.concatenate(ids, axis=1)
            far = half if core == 0 else unit
            level = jnp.where(outer, 3 * far, 1 + far)
            for slot in range(3):
                group = owners[slot]
                if core == 0:
                    keys = theirs[slot * 2 * ROWS : (slot + 1) * 2 * ROWS, :]
                else:
                    b_rows = pl.ds(pl.multiple_of(group % 2 * ROWS, ROWS), ROWS)
                    keys = [mine[4 * unit + 2 * xh + group // 2, b_rows, :] for xh in range(2)]
                    keys = jnp.concatenate(keys, axis=0)
                here = lax.shift_right_logical(ids, 9) == group * 16 + level * 4 + y
                rows = jnp.where(here, ids & 511, -1)
                hit = lax.broadcasted_iota(jnp.int32, (deep, wide), 0) == rows
                logits = lax.dot_general(
                    keys * half_scale, a, (((1,), (1,)), ((), ())), preferred_element_type=jnp.float32
                )
                weights = jnp.tanh(logits + half_bias) + jnp.where(hit, -1.0, 1.0)
                weights = weights.astype(jnp.bfloat16)
                gb = jnp.dot(weights, a, preferred_element_type=jnp.float32)
                ga = lax.dot_general(
                    weights, keys, (((0,), (0,)), ((), ())), preferred_element_type=jnp.float32
                )
                if core == 0:
                    add(sums, slot * 2, gb, unit == 0)
                    add(keep, unit * 4, ga, half == 0 and slot == 0)
                else:
                    add(keep, slot * 4 + unit * 2, gb, half == 0)
                    add(sums, 0, ga, unit == 0 and slot == 0)
        if core == 0:
            powers = encode_all(send, sums)
        else:
            powers = [
                encode(send, i * ROWS, lambda first, last: sums[i, :, first:last]) for i in range(4)
            ]
        send[6 * ROWS :, :] = notes(powers)

    on_core(body)


def pack_kernel(half, plan, keep, got, *refs):
    out, powers = refs[-2:]

    def body(core):
        if core == 0:
            got_powers = got[6 * ROWS :, :].astype(jnp.float32)
        else:
            powers[...] = got[6 * ROWS :, :].astype(jnp.float32)
            own, mate = window(plan, 1), window(plan, 0)
        for i in range(4):
            s = half * 4 + i
            written = []
            if core == 0:
                power = encode(out.at[s], 0, lambda first, last: keep[s, :, first:last])
                out[s, ROWS : 2 * ROWS, :] = got[i * ROWS : (i + 1) * ROWS, :]
                written = [power, got_powers[i : i + 1]]
            else:
                for c in range(2):
                    group, xh = i % 2 * 2 + c, i // 2
                    slot, kept = place_in(own, group)
                    block = slot * 4 + half * 2 + xh
                    slot, used = place_in(mate, group)
                    index = slot * 2 + xh
                    scale = jnp.exp2(powers[pl.ds(index, 1), :] * (1.0 / 128.0)) * (used * (1.0 / PEAK))
                    rows = pl.ds(pl.multiple_of(index * ROWS, ROWS), ROWS)

                    def load(first, last):
                        code = got[rows, first:last].astype(jnp.float32)
                        return keep[block, :, first:last] * kept + code * scale[:, first:last]

                    written.append(encode(out.at[s], c * ROWS, load))
            out[s, 2 * ROWS :, :] = notes(written)

    on_core(body)


def sum_kernel(factor, kept, got, out):
    def body(core):
        c = core if kept else 1 - core
        total = jnp.zeros((ROWS, ROWS), jnp.float32)
        for s in range(8):
            power = got[s, 2 * ROWS :, :].astype(jnp.float32)[c : c + 1]
            total += decode(got[s, c * ROWS : (c + 1) * ROWS, :], power)
        out[...] = total * factor

    on_core(body)


def call(kernel, shapes, scratch, flops, *operands, plan=None, aliases={}):
    operands = operands if plan is None else (plan, *operands)
    return pl.pallas_call(
        kernel,
        out_shape=shapes,
        in_specs=[VMEM] * len(operands),
        out_specs=jax.tree.map(lambda _: VMEM, shapes),
        scratch_shapes=scratch,
        input_output_aliases=aliases,
        compiler_params=pltpu.CompilerParams(vmem_limit_bytes=36 << 20),
        cost_estimate=pl.CostEstimate(flops=flops, bytes_accessed=8 << 20, transcendentals=0),
    )(*operands)


def shards(views_a, views_b, positives, plan):
    factor = logit_scale / math.sqrt(views_a.shape[1])
    f32, i16, bf16 = jnp.float32, jnp.int16, jnp.bfloat16
    height = 2 * ROWS + NOTE
    core = lax.axis_index("core")
    ids = positives.reshape(1, ROWS)
    got = [swap_core(value) for value in (views_a, views_b, ids)]
    own = jnp.where(core == 0, views_a, views_b)
    own_ids = jnp.where(core == 0, ids, 0)
    built = jax.ShapeDtypeStruct((8, height, ROWS), bf16)
    mine = meet(call(build_kernel, built, [], 1 << 10, own, own_ids, *got))
    picked = jax.ShapeDtypeStruct((6 * ROWS, ROWS), bf16)
    near, far = [
        swap_core(call(functools.partial(pick_kernel, half), picked, [], 1 << 10, mine, plan=plan))
        for half in range(2)
    ]

    def score(half, theirs, *keep):
        return call(
            functools.partial(score_kernel, factor, half),
            (
                jax.ShapeDtypeStruct((12, ROWS, ROWS), f32),
                jax.ShapeDtypeStruct((6 * ROWS + NOTE, ROWS), i16),
            ),
            [pltpu.VMEM((6, ROWS, ROWS), f32)],
            3 * 2048 * 3072 * 256,
            mine,
            theirs,
            *keep,
            plan=plan,
            aliases={3: 0} if keep else {},
        )

    def pack(half, keep, got, *packed):
        return call(
            functools.partial(pack_kernel, half),
            jax.ShapeDtypeStruct((8, height, ROWS), i16),
            [pltpu.VMEM((NOTE, ROWS), f32)],
            1 << 20,
            keep,
            got,
            *packed,
            plan=plan,
            aliases={3: 0} if packed else {},
        )

    keep, send_near = score(0, near)
    got_near = swap_core(send_near)
    keep, send_far = score(1, far, keep)
    got_far = swap_core(send_far)
    packed = pack(1, keep, got_far, pack(0, keep, got_near))
    one = jax.ShapeDtypeStruct((ROWS, ROWS), f32)
    pieces = meet(packed)
    send, keep = [
        call(functools.partial(sum_kernel, 0.5 * factor, kept), one, [], 1 << 28, pieces)
        for kept in (False, True)
    ]
    got = swap_core(send)
    return jnp.where(core == 0, keep, got), jnp.where(core == 0, got, keep)


def solution(mesh):
    fine = Mesh(mesh.devices.reshape(2, 2, 4, 4, 2), AXES)
    split = P(AXES, None)
    return jax.shard_map(
        shards,
        mesh=fine,
        in_specs=(split, split, P(AXES), P()),
        out_specs=(split, split),
        check_vma=False,
    )
```
